32 devices in a mesh: dp: 8 (over z, x), tensor: 4 (over y, core).
Axes of the slice: x: 2, y: 2, z: 4, core: 2. Of those that a mesh axis runs over, the one named last changes fastest.
Arguments:
- tokens: bfloat16 [16384, 768], P(('dp', 'tensor')), may hold values from -6 to 6
- segment: int32 [16384], P('dp'), may hold values from 0 to 7, as said below
- cotangent: bfloat16 [16384, 768], P(('dp', 'tensor')), may hold values from -6 to 6
- ln1_gain: float32 [768], replicated, may hold values from 0.5 to 1.5
- ln1_bias: float32 [768], replicated, may hold values from -1.75 to 1.75
- w_qkv: bfloat16 [3, 768, 768], P(None, 'dp', 'tensor'), may hold values from -0.21875 to 0.21875
- qv_bias: bfloat16 [2, 12, 64], P(None, 'tensor', 'dp'), may hold values from -1.75 to 1.75
- w_out: bfloat16 [768, 768], P('tensor', 'dp'), may hold values from -0.875 to 0.875
- out_bias: bfloat16 [768], replicated, may hold values from -1.75 to 1.75
- ln2_gain: float32 [768], replicated, may hold values from 0.5 to 1.5
- ln2_bias: float32 [768], replicated, may hold values from -1.75 to 1.75
- w_up: bfloat16 [768, 3072], P('dp', 'tensor'), may hold values from -0.21875 to 0.21875
- up_bias: bfloat16 [48, 64], P('tensor', 'dp'), may hold values from -1.75 to 1.75
- w_down: bfloat16 [3072, 768], P('tensor', 'dp'), may hold values from -0.109375 to 0.109375
- down_bias: bfloat16 [768], replicated, may hold values from -1.75 to 1.75
Outputs:
- block_out: float32 [16384, 768], P(('dp', 'tensor'))
- tokens_grad: float32 [16384, 768], P(('dp', 'tensor'))
- ln1_gain_grad: float32 [768], replicated
- ln1_bias_grad: float32 [768], replicated
- w_qkv_grad: float32 [3, 768, 768], P(None, 'dp', 'tensor')
- qv_bias_grad: float32 [2, 12, 64], P(None, 'tensor', 'dp')
- w_out_grad: float32 [768, 768], P('tensor', 'dp')
- out_bias_grad: float32 [768], replicated
- ln2_gain_grad: float32 [768], replicated
- ln2_bias_grad: float32 [768], replicated
- w_up_grad: float32 [768, 3072], P('dp', 'tensor')
- up_bias_grad: float32 [48, 64], P('tensor', 'dp')
- w_down_grad: float32 [3072, 768], P('tensor', 'dp')
- down_bias_grad: float32 [768], replicated
The draws below stay inside these ranges and needn't reach their ends.
Inputs may be any that keep to these rules, and one draw needn't show every extreme that they name: Within each packed row of 2048 tokens the segment numbers start at 0, never fall and end at 7, each taken by one run of tokens; one document of each row starts within the row's first 512 tokens and ends within its last 512.
All inputs are finite; a program needn't handle non-finite values.
Results may differ from the reference program's by a relative error of at most 0.0096.
Values may be sent and summed in bfloat16 or wider, within the bound.
No kernel may reach another device: no remote copies, remote signals or barrier semaphores. Data moves between devices by JAX's collectives and lax.ppermute only.
A program may use at most 128 MiB of HBM per device.

```python
from functools import partial
import jax
import jax.numpy as jnp
from jax import lax

D = 768
HEADS = 12
HD = 64
FF = 3072
ROW_TOK = 2048
QBLK = 512
DOCS = 8
TOKENS = 16384
TOK_DEV = 512


def draw_segment(key, part):
    key = jax.random.fold_in(key, 11)
    key_list = jax.random.split(key, 3)
    row_count = TOKENS // ROW_TOK
    long_doc = jax.random.randint(key_list[0], (row_count, 1), 0, DOCS - 1)
    start_at = long_doc + jax.random.randint(key_list[1], (row_count, 1), 0, TOK_DEV // 2)
    after_count = DOCS - 1 - long_doc
    finish_at = ROW_TOK - after_count - jax.random.randint(key_list[2], (row_count, 1), 0, TOK_DEV // 2)
    position = jnp.arange(ROW_TOK, dtype=jnp.int32)[None, :]
    before_id = long_doc * position // jnp.maximum(start_at, 1)
    after_id = long_doc + 1 + after_count * (position - finish_at) // (ROW_TOK - finish_at)
    segment_id = jnp.where(position < start_at, before_id, jnp.where(position < finish_at, long_doc, after_id))
    return segment_id.reshape(TOKENS).astype(jnp.int32)


def block_levels(rng, dims, cuts, low, top_value):
    gain = 1.0
    for dim, parts in cuts:
        draws = jax.random.uniform(jax.random.fold_in(jax.random.fold_in(rng, 6), dim), (parts,), jnp.float32, low / len(cuts), top_value / len(cuts))
        gain = gain * jnp.repeat(jnp.exp(draws), dims[dim] // parts).reshape((-1,) + (1,) * (len(dims) - 1 - dim))
    return gain


def noise(rng, shape, spread, reach, cuts=(), kind=jnp.bfloat16):
    array = spread * jax.random.normal(rng, shape, jnp.float32)
    if cuts:
        array = array * block_levels(rng, shape, cuts, -0.22, 0.18)
    return jnp.clip(array, -reach, reach).astype(kind)


def setup_inputs(seed: int = 0) -> dict:
    key_of = jax.random.split(jax.random.key(seed), 16)
    tokens = noise(key_of[0], (TOKENS, D), 1.0, 6.0, ((0, 32),))
    segment = draw_segment(jax.random.fold_in(key_of[15], 71), 0)
    cotangent = noise(key_of[2], (TOKENS, D), 1.0, 6.0, ((0, 32),))
    ln1_gain = jnp.clip(1.0 + 0.1 * jax.random.normal(key_of[3], (D,), jnp.float32), 0.5, 1.5)
    ln1_bias = noise(key_of[4], (D,), 0.3, 1.75, (), jnp.float32)
    w_qkv = noise(key_of[5], (3, D, D), D ** -0.5, 0.21875, ((1, 8), (2, 4)))
    qv_bias = noise(key_of[6], (2, HEADS, HD), 0.3, 1.75, ((1, 4), (2, 8)))
    w_out = noise(key_of[7], (D, D), (D // 16) ** -0.5, 0.875, ((0, 4), (1, 8)))
    out_bias = noise(key_of[8], (D,), 0.3, 1.75)
    ln2_gain = jnp.clip(1.0 + 0.1 * jax.random.normal(key_of[9], (D,), jnp.float32), 0.5, 1.5)
    ln2_bias = noise(key_of[10], (D,), 0.3, 1.75, (), jnp.float32)
    w_up = noise(key_of[11], (D, FF), D ** -0.5, 0.21875, ((0, 8), (1, 4)))
    up_bias = noise(key_of[12], (FF // HD, HD), 0.3, 1.75, ((0, 4), (1, 8)))
    w_down = noise(key_of[13], (FF, D), FF ** -0.5, 0.109375, ((0, 4), (1, 8)))
    down_bias = noise(key_of[14], (D,), 0.3, 1.75)
    return dict(tokens=tokens, segment=segment, cotangent=cotangent, ln1_gain=ln1_gain, ln1_bias=ln1_bias, w_qkv=w_qkv, qv_bias=qv_bias, w_out=w_out, out_bias=out_bias, ln2_gain=ln2_gain, ln2_bias=ln2_bias, w_up=w_up, up_bias=up_bias, w_down=w_down, down_bias=down_bias)


@jax.custom_vjp
def low(v):
    return lax.optimization_barrier(v.astype(jnp.bfloat16)).astype(jnp.float32)

@jax.custom_vjp
def low_back(v):
    return v

def low_keep(v):
    return (low(v), None)

def low_pass(kept, grad):
    return (grad,)

def back_keep(v):
    return (v, None)

def back_low(kept, grad):
    return (low(grad),)
low.defvjp(low_keep, low_pass)
low_back.defvjp(back_keep, back_low)
HIGHEST = lax.Precision.HIGHEST
EPSILON = 1e-05
GELU_COEF = 0.7978845608028654

def layer_norm(values_in, gain_vec, shift_vec):
    row_mean = lax.optimization_barrier(jnp.mean(values_in, axis=-1, keepdims=True))
    centered = values_in - row_mean
    variance = lax.optimization_barrier(jnp.mean(centered * centered, axis=-1, keepdims=True))
    return centered * lax.rsqrt(variance + EPSILON) * gain_vec + shift_vec

def gelu_tanh(values_in):
    return 0.5 * values_in * (1.0 + jnp.tanh(GELU_COEF * (values_in + 0.044715 * values_in * values_in * values_in)))

def matmul(left_mat, right_mat):
    return jnp.dot(left_mat, right_mat, precision=HIGHEST)

def attend_row(packed):
    query_rows, key_rows, value_rows, segment_row = packed
    position = jnp.arange(ROW_TOK, dtype=jnp.int32)
    score_scale = HD ** (-0.5)

    def one_block(block_start):
        query_block = lax.dynamic_slice_in_dim(query_rows, block_start, QBLK, 0)
        segment_block = lax.dynamic_slice_in_dim(segment_row, block_start, QBLK, 0)
        position_block = block_start + jnp.arange(QBLK, dtype=jnp.int32)
        raw_scores = jnp.einsum('qhd,khd->hqk', query_block, key_rows, precision=HIGHEST) * score_scale
        scores = low_back(raw_scores)
        allowed = (position[None, :] <= position_block[:, None]) & (segment_row[None, :] == segment_block[:, None])
        scores = jnp.where(allowed[None, :, :], scores, -1e+30)
        row_max = lax.optimization_barrier(jnp.max(scores, axis=-1, keepdims=True))
        exponent = jnp.exp(scores - row_max)
        weights_soft = exponent / lax.optimization_barrier(jnp.sum(exponent, axis=-1, keepdims=True))
        return jnp.einsum('hqk,khd->qhd', low(weights_soft), value_rows, precision=HIGHEST)
    block_starts = jnp.arange(ROW_TOK // QBLK, dtype=jnp.int32) * QBLK
    mixed_heads = lax.map(jax.checkpoint(one_block), block_starts)
    return mixed_heads.reshape(ROW_TOK, HEADS * HD)

def forward(segment, tokens, ln1_gain, ln1_bias, w_qkv, qv_bias, w_out, out_bias, ln2_gain, ln2_bias, w_up, up_bias, w_down, down_bias):
    first_norm = low(layer_norm(tokens, ln1_gain, ln1_bias))
    queries = low(low_back(matmul(first_norm, w_qkv[0]) + qv_bias[0].reshape(D)))
    keys_all = low(low_back(matmul(first_norm, w_qkv[1])))
    values_all = low(low_back(matmul(first_norm, w_qkv[2]) + qv_bias[1].reshape(D)))
    row_count = TOKENS // ROW_TOK

    def per_row(array_in):
        return array_in.reshape(row_count, ROW_TOK, HEADS, HD)
    heads_out = lax.map(attend_row, (per_row(queries), per_row(keys_all), per_row(values_all), segment.reshape(row_count, ROW_TOK)))
    heads_out = low(low_back(heads_out.reshape(TOKENS, D)))
    hidden_one = tokens + low_back(matmul(heads_out, w_out) + out_bias)
    second = low(layer_norm(hidden_one, ln2_gain, ln2_bias))
    pre_act = low_back(matmul(second, w_up) + up_bias.reshape(FF))
    activation = low(gelu_tanh(pre_act))
    return hidden_one + low_back(matmul(activation, w_down) + down_bias)

def reference(tokens, segment, cotangent, ln1_gain, ln1_bias, w_qkv, qv_bias, w_out, out_bias, ln2_gain, ln2_bias, w_up, up_bias, w_down, down_bias):
    params = [array_in.astype(jnp.float32) for array_in in (tokens, ln1_gain, ln1_bias, w_qkv, qv_bias, w_out, out_bias, ln2_gain, ln2_bias, w_up, up_bias, w_down, down_bias)]
    block_out, pull_back = jax.vjp(partial(forward, segment), *params)
    gradients = pull_back(cotangent.astype(jnp.float32))
    return (block_out, gradients[0], gradients[1], gradients[2], gradients[3], gradients[4], gradients[5], gradients[6], gradients[7], gradients[8], gradients[9], gradients[10], gradients[11], gradients[12])
```

```python
import jax
import jax.numpy as jnp
from jax import lax
from jax.experimental import pallas as pl
from jax.experimental.pallas import tpu as pltpu
from jax.sharding import PartitionSpec as P

HD = 64
BLK = 256
EDGE = 512
FEW = 8
EPSILON = 1e-05
GELU_COEF = 0.7978845608028654
NT = (((1,), (1,)), ((), ()))
TN = (((0,), (0,)), ((), ()))
NN = (((1,), (0,)), ((), ()))


def dot32(left, right, dims):
    return lax.dot_general(left, right, dims, preferred_element_type=jnp.float32)


def one_document(row_total, block_a, block_b):
    low, high = EDGE // BLK, (row_total - EDGE) // BLK
    return low <= block_a < high and low <= block_b < high


def split_heads(source, first, scratch, heads, scale=None):
    for h in range(heads):
        part = source[:, first + h * HD : first + (h + 1) * HD]
        scratch[h] = part if scale is None else (part.astype(jnp.float32) * scale).astype(jnp.bfloat16)


def attend_kernel(qkv, seg_col, seg_row, out, lse, q_s, k_s, v_s, o_s, c_s):
    rows, width = out.shape
    heads = width // HD
    split_heads(qkv, 0, q_s, heads, HD ** -0.5)
    split_heads(qkv, width, k_s, heads)
    split_heads(qkv, 2 * width, v_s, heads)
    c_s[...] = jnp.broadcast_to(seg_col[...], (rows, 128))

    @pl.loop(0, heads)
    def _(h):
        for i in range(rows // BLK):
            mine = pl.ds(i * BLK, BLK)
            query = q_s[h, mine, :]
            seg_mine = c_s[mine, :]
            seg_mine = jnp.concatenate([seg_mine, seg_mine], axis=1)
            tiles = []
            for j in range(i + 1):
                other = pl.ds(j * BLK, BLK)
                score = dot32(query, k_s[h, other, :], NT)
                allowed = None
                if not one_document(rows, i, j):
                    allowed = seg_mine == seg_row[:, other]
                if i == j:
                    causal = lax.broadcasted_iota(jnp.int32, (BLK, BLK), 1) <= lax.broadcasted_iota(
                        jnp.int32, (BLK, BLK), 0
                    )
                    allowed = causal if allowed is None else allowed & causal
                if allowed is not None:
                    score = jnp.where(allowed, score, -1e30)
                tiles.append(score)
            top = tiles[0]
            for tile in tiles[1:]:
                top = jnp.maximum(top, tile)
            top = jnp.max(top, axis=1, keepdims=True)
            total = None
            mixed = None
            for j, tile in enumerate(tiles):
                weight = jnp.exp(tile - top)
                total = weight if total is None else total + weight
                term = dot32(weight.astype(jnp.bfloat16), v_s[h, pl.ds(j * BLK, BLK), :], NN)
                mixed = term if mixed is None else mixed + term
            total = jnp.sum(total, axis=1, keepdims=True)
            o_s[h, mine, :] = (mixed / total).astype(jnp.bfloat16)
            log_total = jnp.broadcast_to(top + jnp.log(total), (BLK, 128))
            lse[h, :, mine] = jnp.transpose(log_total)[0:8, :]

    for h in range(heads):
        out[:, h * HD : (h + 1) * HD] = o_s[h]


def attend(qkv, segment):
    rows = qkv.shape[0]
    width = qkv.shape[1] // 3
    heads = width // HD
    return pl.pallas_call(
        attend_kernel,
        out_shape=(
            jax.ShapeDtypeStruct((rows, width), jnp.bfloat16),
            jax.ShapeDtypeStruct((heads, 8, rows), jnp.float32),
        ),
        scratch_shapes=[pltpu.VMEM((heads, rows, HD), jnp.bfloat16)] * 4
        + [pltpu.VMEM((rows, 128), jnp.int32)],
        compiler_params=pltpu.CompilerParams(vmem_limit_bytes=48 * 2**20),
        cost_estimate=pl.CostEstimate(
            flops=heads * rows * rows * HD * 4, bytes_accessed=rows * width * 8, transcendentals=heads * rows * rows // 2
        ),
        name="attend",
    )(qkv, segment[:, None], segment[None, :])


def attend_back_kernel(
    qkv, mixed, grad, lse, seg_col, seg_row, out, q_s, k_s, v_s, g_s, d_s, dq_s, dk_s, dv_s, c_s
):
    rows, width = mixed.shape
    heads = width // HD
    split_heads(qkv, 0, q_s, heads, HD ** -0.5)
    split_heads(qkv, width, k_s, heads)
    split_heads(qkv, 2 * width, v_s, heads)
    split_heads(grad, 0, g_s, heads)
    c_s[...] = jnp.broadcast_to(seg_col[...], (rows, 128))
    for h in range(heads):
        both = mixed[:, h * HD : (h + 1) * HD].astype(jnp.float32) * g_s[h].astype(jnp.float32)
        inner = jnp.sum(both, axis=1, keepdims=True)
        d_s[h] = jnp.transpose(jnp.broadcast_to(inner, (rows, 128)))[0:8, :]

    @pl.loop(0, heads)
    def _(h):
        for i in range(rows // BLK):
            mine = pl.ds(i * BLK, BLK)
            query = q_s[h, mine, :]
            grad_mine = g_s[h, mine, :]
            log_total = lse[h, 0:1, mine]
            inner = d_s[h, 0:1, mine]
            query_grad = None
            for j in range(i + 1):
                other = pl.ds(j * BLK, BLK)
                key = k_s[h, other, :]
                score = dot32(key, query, NT)
                weight = jnp.exp(score - log_total)
                allowed = None
                if not one_document(rows, i, j):
                    seg_other = c_s[other, :]
                    seg_other = jnp.concatenate([seg_other, seg_other], axis=1)
                    allowed = seg_other == seg_row[:, mine]
                if i == j:
                    causal = lax.broadcasted_iota(jnp.int32, (BLK, BLK), 0) <= lax.broadcasted_iota(
                        jnp.int32, (BLK, BLK), 1
                    )
                    allowed = causal if allowed is None else allowed & causal
                if allowed is not None:
                    weight = jnp.where(allowed, weight, 0.0)
                weight_grad = dot32(v_s[h, other, :], grad_mine, NT)
                score_grad = (weight * (weight_grad - inner)).astype(jnp.bfloat16)
                value_term = dot32(weight.astype(jnp.bfloat16), grad_mine, NN)
                key_term = dot32(score_grad, query, NN)
                query_term = dot32(score_grad, key, TN)
                query_grad = query_term if query_grad is None else query_grad + query_term
                if i == j:
                    dv_s[h, other, :] = value_term
                    dk_s[h, other, :] = key_term
                else:
                    dv_s[h, other, :] += value_term
                    dk_s[h, other, :] += key_term
            dq_s[h, mine, :] = (query_grad * HD ** -0.5).astype(jnp.bfloat16)

    for h in range(heads):
        out[:, h * HD : (h + 1) * HD] = dq_s[h]
        out[:, width + h * HD : width + (h + 1) * HD] = dk_s[h].astype(jnp.bfloat16)
        out[:, 2 * width + h * HD : 2 * width + (h + 1) * HD] = dv_s[h].astype(jnp.bfloat16)


def attend_back(qkv, mixed, grad, lse, segment):
    rows = qkv.shape[0]
    width = qkv.shape[1] // 3
    heads = width // HD
    half = pltpu.VMEM((heads, rows, HD), jnp.bfloat16)
    full = pltpu.VMEM((heads, rows, HD), jnp.float32)
    return pl.pallas_call(
        attend_back_kernel,
        out_shape=jax.ShapeDtypeStruct((rows, 3 * width), jnp.bfloat16),
        scratch_shapes=[half, half, half, half, pltpu.VMEM((heads, 8, rows), jnp.float32), half, full, full]
        + [pltpu.VMEM((rows, 128), jnp.int32)],
        compiler_params=pltpu.CompilerParams(vmem_limit_bytes=48 * 2**20),
        cost_estimate=pl.CostEstimate(
            flops=heads * rows * rows * HD * 10, bytes_accessed=rows * width * 16, transcendentals=heads * rows * rows // 2
        ),
        name="attend_back",
    )(qkv, mixed, grad, lse, segment[:, None], segment[None, :])


def flip(values, axis, mask):
    size = lax.axis_size(axis)
    return lax.ppermute(values, axis, [(i, i ^ mask) for i in range(size)])


def core_swap(values):
    return flip(values, "tensor", 1)


def chip_swap(values):
    return flip(values, "tensor", 2)


def place(buffer, piece, index):
    return lax.dynamic_update_slice_in_dim(buffer, piece[None], index, 0)


def pick(blocks, index):
    return lax.dynamic_index_in_dim(blocks, index, 0, keepdims=False)


def gather_direct(shard, axis):
    size = lax.axis_size(axis)
    if size > FEW:
        return lax.all_gather(shard, axis)
    me = lax.axis_index(axis)
    whole = place(jnp.zeros((size,) + shard.shape, shard.dtype), shard, me)
    for mask in range(1, size):
        whole = place(whole, flip(shard, axis, mask), me ^ mask)
    return whole


def gather_two(shard):
    size = lax.axis_size("dp")
    if size > FEW:
        return lax.all_gather(shard, "dp", tiled=True)
    me = lax.axis_index("dp")
    column = place(jnp.zeros((size // 2,) + shard.shape, shard.dtype), shard, me // 2)
    for mask in range(2, size, 2):
        column = place(column, flip(shard, "dp", mask), (me ^ mask) // 2)
    other = flip(column, "dp", 1)
    whole = jnp.zeros((size // 2, 2) + shard.shape, shard.dtype)
    whole = lax.dynamic_update_slice_in_dim(whole, column[:, None], me % 2, 1)
    whole = lax.dynamic_update_slice_in_dim(whole, other[:, None], 1 - me % 2, 1)
    return whole.reshape((size * shard.shape[0],) + shard.shape[1:])


def scatter_all(whole, axis):
    blocks = low(whole).reshape((lax.axis_size(axis), -1) + whole.shape[1:])
    return jnp.sum(wide(lax.all_to_all(blocks, axis, 0, 0, tiled=True)), axis=0)


def scatter_direct(whole, axis):
    size = lax.axis_size(axis)
    if size > FEW:
        return scatter_all(whole, axis)
    me = lax.axis_index(axis)
    blocks = whole.reshape((size, -1) + whole.shape[1:])
    total = pick(blocks, me).astype(jnp.float32)
    low = blocks.astype(jnp.bfloat16)
    for mask in range(1, size):
        total = total + flip(pick(low, me ^ mask), axis, mask).astype(jnp.float32)
    return total


def scatter_two(whole):
    size = lax.axis_size("dp")
    if size > FEW:
        return scatter_all(whole, "dp")
    me = lax.axis_index("dp")
    blocks = whole.reshape((size // 2, 2, -1) + whole.shape[1:])
    keep = lax.dynamic_index_in_dim(blocks, me % 2, 1, keepdims=False)
    give = lax.dynamic_index_in_dim(blocks, 1 - me % 2, 1, keepdims=False)
    column = keep.astype(jnp.float32) + flip(give.astype(jnp.bfloat16), "dp", 1).astype(jnp.float32)
    total = pick(column, me // 2)
    low = column.astype(jnp.bfloat16)
    for mask in range(2, size, 2):
        total = total + flip(pick(low, (me ^ mask) // 2), "dp", mask).astype(jnp.float32)
    return total


def sum_everywhere(values):
    for mask in (1, 2):
        values = values + flip(values, "tensor", mask)
    mask = 1
    while mask < lax.axis_size("dp"):
        values = values + flip(values, "dp", mask)
        mask *= 2
    return values


def normalized(values_in):
    row_mean = jnp.mean(values_in, axis=-1, keepdims=True)
    centered = values_in - row_mean
    variance = jnp.mean(centered * centered, axis=-1, keepdims=True)
    return centered * lax.rsqrt(variance + EPSILON)


def layer_norm(values_in, gain_vec, shift_vec):
    return normalized(values_in) * gain_vec + shift_vec


def gelu_tanh(values_in):
    return (
        0.5
        * values_in
        * (1.0 + jnp.tanh(GELU_COEF * (values_in + 0.044715 * values_in * values_in * values_in)))
    )


def product(left_mat, right_mat):
    return jnp.dot(left_mat, right_mat, preferred_element_type=jnp.float32)


def contract_rows(left_mat, right_mat):
    return lax.dot_general(left_mat, right_mat, TN, preferred_element_type=jnp.float32)


def contract_cols(left_mat, right_mat):
    return lax.dot_general(left_mat, right_mat, NT, preferred_element_type=jnp.float32)


def low(values):
    return values.astype(jnp.bfloat16)


def wide(values):
    return values.astype(jnp.float32)


def on_device(
    tokens,
    segment,
    cotangent,
    ln1_gain,
    ln1_bias,
    w_qkv,
    qv_bias,
    w_out,
    out_bias,
    ln2_gain,
    ln2_bias,
    w_up,
    up_bias,
    w_down,
    down_bias,
):
    dp = lax.axis_size("dp")
    place_dp = lax.axis_index("dp")
    me = lax.axis_index("tensor")
    own, width = tokens.shape
    rows_shard = w_qkv.shape[1]
    span = w_qkv.shape[2]
    hidden = w_up.shape[1]

    biases = jnp.concatenate([qv_bias.reshape(-1), up_bias.reshape(-1)])
    bias_rows = jnp.zeros((16, 3 * span), jnp.bfloat16).at[0, : biases.shape[0]].set(biases)
    pack = jnp.concatenate([jnp.swapaxes(w_qkv, 0, 1).reshape(rows_shard, 3 * span), bias_rows], axis=0)
    packs = gather_direct(pack, "dp")
    qkv_full = packs[:, :rows_shard].reshape(dp * rows_shard, 3 * span)
    bias_parts = packs[:, rows_shard, : biases.shape[0]]
    qv_full = jnp.moveaxis(bias_parts[:, : qv_bias.size].reshape((dp,) + qv_bias.shape), 0, 2).reshape(2, span)
    up_bias_own = jnp.moveaxis(
        bias_parts[:, qv_bias.size :].reshape((dp,) + up_bias.shape), 0, 1
    ).reshape(hidden)
    up_bias_pair = wide(jnp.concatenate([up_bias_own, chip_swap(up_bias_own)]))

    from_chip = chip_swap(tokens)
    token_pieces = [tokens, core_swap(tokens), from_chip, core_swap(from_chip)]
    first_norm = jnp.zeros((4, own, width), jnp.bfloat16)
    for mask, piece in enumerate(token_pieces):
        first_norm = place(first_norm, low(layer_norm(wide(piece), ln1_gain, ln1_bias)), me ^ mask)
    first_norm = first_norm.reshape(4 * own, width)
    qkv_bias = wide(jnp.concatenate([qv_full[0], jnp.zeros_like(qv_full[0]), qv_full[1]]))
    qkv = low(product(first_norm, qkv_full) + qkv_bias)

    out_t = gather_direct(w_out.T, "dp").reshape(dp * rows_shard, span)
    out_own = out_t.T
    out_chip = chip_swap(out_own)
    out_near = jnp.concatenate([out_own, core_swap(out_own)], axis=0)
    out_far = jnp.concatenate([out_chip, core_swap(out_chip)], axis=0)
    up_pair = gather_two(jnp.concatenate([w_up, chip_swap(w_up)], axis=1))
    down_own = gather_two(w_down.T)
    down_chip = chip_swap(down_own)
    grad_pair = jnp.concatenate([cotangent, core_swap(cotangent)], axis=0)

    heads_out, log_totals = attend(qkv, segment)

    blocks = heads_out.reshape(4, own, span)
    to_core = jnp.stack([pick(blocks, me ^ 1), pick(blocks, me ^ 3)])
    from_core = core_swap(to_core)
    mixed_near = jnp.concatenate([pick(blocks, me), from_core[0]], axis=1)
    mixed_far = chip_swap(jnp.concatenate([pick(blocks, me ^ 2), from_core[1]], axis=1))
    token_rows = wide(tokens)
    attn_branch = product(mixed_near, out_near) + product(mixed_far, out_far)
    hidden_one = token_rows + (attn_branch + wide(out_bias))

    second_own = low(layer_norm(hidden_one, ln2_gain, ln2_bias))
    second = jnp.concatenate([second_own, core_swap(second_own)], axis=0)
    pre_act = product(second, up_pair) + up_bias_pair
    activation = low(gelu_tanh(pre_act))
    act_grad = jnp.concatenate([product(grad_pair, down_own), product(grad_pair, down_chip)], axis=1)
    pre_grad = low(jax.vjp(gelu_tanh, pre_act)[1](act_grad)[0])
    second_part = contract_cols(pre_grad, up_pair)
    second_grad = second_part[:own] + wide(core_swap(low(second_part[own:])))
    norm_pull = jax.vjp(layer_norm, hidden_one, ln2_gain, ln2_bias)[1]
    hidden_grad_norm, ln2_gain_grad, ln2_bias_grad = norm_pull(second_grad)
    hidden_grad = wide(cotangent) + hidden_grad_norm

    mlp_part = contract_cols(activation[:, :hidden], down_own) + contract_cols(activation[:, hidden:], down_chip)
    mlp_branch = mlp_part[:own] + wide(core_swap(low(mlp_part[own:])))
    block_out = hidden_one + (mlp_branch + wide(down_bias))

    down_part = scatter_two(contract_rows(grad_pair, activation))
    down_grad_out = (down_part[:, :hidden] + wide(chip_swap(low(down_part[:, hidden:])))).T
    up_part = contract_rows(second, pre_grad)
    up_grad_out = scatter_two(up_part[:, :hidden] + wide(chip_swap(low(up_part[:, hidden:]))))

    grad_attn = low(hidden_grad)
    grad_near = low(contract_cols(grad_attn, out_near))
    grad_far = chip_swap(low(contract_cols(grad_attn, out_far)))
    grad_core = core_swap(jnp.stack([grad_near[:, span:], grad_far[:, span:]]))
    heads_grad = jnp.zeros((4, own, span), jnp.bfloat16)
    for mask, piece in enumerate((grad_near[:, :span], grad_core[0], grad_far[:, :span], grad_core[1])):
        heads_grad = place(heads_grad, piece, me ^ mask)
    heads_grad = heads_grad.reshape(4 * own, span)

    out_part_near = contract_rows(mixed_near, grad_attn)
    out_part_far = contract_rows(mixed_far, grad_attn)
    out_core = core_swap(low(jnp.stack([out_part_near[span:], out_part_far[span:]])))
    out_grad = out_part_near[:span] + wide(out_core[0])
    out_grad = out_grad + wide(chip_swap(low(out_part_far[:span] + wide(out_core[1]))))
    w_out_grad_out = scatter_direct(out_grad.T, "dp").T

    up_bias_sum = jnp.sum(wide(pre_grad), axis=0)
    up_bias_rows = jnp.zeros((4, hidden), jnp.float32)
    up_bias_rows = place(up_bias_rows, up_bias_sum[:hidden], me)
    up_bias_rows = place(up_bias_rows, up_bias_sum[hidden:], me ^ 2)
    early = lax.psum(
        jnp.concatenate(
            [
                jnp.stack(
                    [
                        jnp.sum(wide(grad_attn), axis=0),
                        ln2_gain_grad,
                        ln2_bias_grad,
                        jnp.sum(wide(cotangent), axis=0),
                    ]
                ).reshape(-1),
                up_bias_rows.reshape(-1),
            ]
        ),
        ("dp", "tensor"),
    )
    vectors = early[: 4 * width].reshape(4, width)
    up_bias_grad = pick(early[4 * width :].reshape((4,) + (up_bias.shape[0], dp, up_bias.shape[1])), me)
    up_bias_grad = lax.dynamic_index_in_dim(up_bias_grad, place_dp, 1, keepdims=False)

    qkv_grad = attend_back(qkv, heads_out, heads_grad, log_totals, segment)

    grad_blocks = qkv_grad.reshape(4, own, 3 * span)
    parts = [None] * 4
    for mask in (3, 2, 1, 0):
        parts[mask] = contract_cols(pick(grad_blocks, me ^ mask), qkv_full)
    first_grad_chip = chip_swap(low(parts[2] + wide(core_swap(low(parts[3])))))
    first_grad = parts[0] + wide(core_swap(low(parts[1]))) + wide(first_grad_chip)
    qkv_sum = scatter_direct(contract_rows(first_norm, qkv_grad), "dp")
    w_qkv_grad_out = jnp.swapaxes(qkv_sum.reshape(rows_shard, 3, span), 0, 1)

    ln1_gain_part = 0.0
    ln1_bias_part = 0.0
    for part, piece in zip(parts, token_pieces):
        ln1_gain_part = ln1_gain_part + jnp.sum(part * normalized(wide(piece)), axis=0)
        ln1_bias_part = ln1_bias_part + jnp.sum(part, axis=0)
    qkv_bias_sum = jnp.sum(wide(qkv_grad), axis=0).reshape(3, span)
    bias_spread = jnp.zeros((4, 2, span), jnp.float32)
    bias_spread = place(bias_spread, jnp.stack([qkv_bias_sum[0], qkv_bias_sum[2]]), me)
    late = sum_everywhere(
        jnp.concatenate([ln1_gain_part, ln1_bias_part, bias_spread.reshape(-1)]).reshape(4, -1)
    ).reshape(-1)
    qv_bias_grad = pick(late[2 * width :].reshape((4, 2, qv_bias.shape[1], dp, qv_bias.shape[2])), me)
    qv_bias_grad = lax.dynamic_index_in_dim(qv_bias_grad, place_dp, 2, keepdims=False)

    first_pull = jax.vjp(lambda v: layer_norm(v, ln1_gain, ln1_bias), token_rows)[1]
    token_grad = hidden_grad + first_pull(first_grad)[0]
    return (
        block_out,
        token_grad,
        late[:width],
        late[width : 2 * width],
        w_qkv_grad_out,
        qv_bias_grad,
        w_out_grad_out,
        vectors[0],
        vectors[1],
        vectors[2],
        up_grad_out,
        up_bias_grad,
        down_grad_out,
        vectors[3],
    )


def solution(mesh):
    in_specs = (
        P(("dp", "tensor"), None),
        P("dp"),
        P(("dp", "tensor"), None),
        P(),
        P(),
        P(None, "dp", "tensor"),
        P(None, "tensor", "dp"),
        P("tensor", "dp"),
        P(),
        P(),
        P(),
        P("dp", "tensor"),
        P("tensor", "dp"),
        P("tensor", "dp"),
        P(),
    )
    out_specs = (
        P(("dp", "tensor"), None),
        P(("dp", "tensor"), None),
        P(),
        P(),
        P(None, "dp", "tensor"),
        P(None, "tensor", "dp"),
        P("tensor", "dp"),
        P(),
        P(),
        P(),
        P("dp", "tensor"),
        P("tensor", "dp"),
        P("tensor", "dp"),
        P(),
    )
    return jax.shard_map(
        on_device, mesh=mesh, in_specs=in_specs, out_specs=out_specs, check_vma=False
    )
```

```python
import functools

import jax
import jax.numpy as jnp
from jax import lax
from jax.experimental import pallas as pl
from jax.experimental.layout import Layout, with_layout_constraint
from jax.experimental.pallas import tpu as pltpu
from jax.sharding import PartitionSpec as P

HD = 64
BLK = 256
EDGE = 512
FEW = 8
PAD = 16
EPSILON = 1e-05
GELU_COEF = 0.7978845608028654
NT = (((1,), (1,)), ((), ()))
TN = (((0,), (0,)), ((), ()))
NN = (((1,), (0,)), ((), ()))
ROOM = pltpu.CompilerParams(vmem_limit_bytes=48 * 2**20)
SCALAR = pl.BlockSpec(memory_space=pltpu.SMEM)
ANYWHERE = pl.BlockSpec(memory_space=pl.ANY)


def low(values):
    return values.astype(jnp.bfloat16)


def wide(values):
    return values.astype(jnp.float32)


def shape16(*dims):
    return jax.ShapeDtypeStruct(dims, jnp.bfloat16)


def shape32(*dims):
    return jax.ShapeDtypeStruct(dims, jnp.float32)


def cost(flops, size, exps=0):
    return pl.CostEstimate(flops=1, bytes_accessed=1, transcendentals=0)


def dot32(left, right, dims):
    return lax.dot_general(left, right, dims, preferred_element_type=jnp.float32)


def normalized(values_in):
    row_mean = jnp.mean(values_in, axis=-1, keepdims=True)
    centered = values_in - row_mean
    variance = jnp.mean(centered * centered, axis=-1, keepdims=True)
    scale = lax.rsqrt(variance + EPSILON)
    return centered * scale, scale


def norm_back(normed, scale, grad):
    mean_grad = jnp.mean(grad, axis=-1, keepdims=True)
    mean_both = jnp.mean(grad * normed, axis=-1, keepdims=True)
    return scale * (grad - mean_grad - normed * mean_both)


def first_kernel(index, piece, gain, shift, *rest):
    normed, _ = normalized(wide(piece[...]))
    rest[-2][0] = low(normed * gain[...] + shift[...])
    rest[-1][...] = low(normed)


def first_norm_of(piece, gain, shift, index, dep, buffer=None):
    own, width = piece.shape
    steps = 2
    rows = own // steps
    row_spec = pl.BlockSpec((1, width), lambda i, at: (0, 0))
    operands = [index.reshape(1), piece, gain[None], shift[None], dep]
    in_specs = [pl.BlockSpec((rows, width), lambda i, at: (i, 0)), row_spec, row_spec, ANYWHERE]
    aliases = {}
    if buffer is not None:
        operands.append(buffer)
        in_specs.append(ANYWHERE)
        aliases = {5: 0}
    return pl.pallas_call(
        first_kernel,
        grid_spec=pltpu.PrefetchScalarGridSpec(
            num_scalar_prefetch=1,
            grid=(steps,),
            in_specs=in_specs,
            out_specs=[
                pl.BlockSpec((1, rows, width), lambda i, at: (at[0], i, 0)),
                pl.BlockSpec((rows, width), lambda i, at: (i, 0)),
            ],
        ),
        out_shape=(shape16(4, own, width), shape16(own, width)),
        input_output_aliases=aliases,
        cost_estimate=cost(own * width * 12, own * width * 4),
        name="first_norm",
    )(*operands)


def pack_kernel(*refs):
    out = refs[-1]
    at = 0
    for ref in refs[:-2]:
        out[:, at : at + ref.shape[1]] = ref[...]
        at += ref.shape[1]
    out[:, at:] = jnp.zeros((out.shape[0], out.shape[1] - at), out.dtype)
    tail = refs[-2]
    count = min(tail.shape[0], out.shape[0])
    out[:count, at : at + tail.shape[1]] = tail[:count, :]


def pack_heads_kernel(weights, tail, out):
    kinds, height, span = weights.shape
    for h in range(span // HD):
        for k in range(kinds):
            at = (h * kinds + k) * HD
            out[:, at : at + HD] = weights[k, :, h * HD : (h + 1) * HD]
    out[:, kinds * span :] = jnp.zeros((height, tail.shape[1]), out.dtype)
    count = min(tail.shape[0], height)
    out[:count, kinds * span :] = tail[:count, :]


def pack(arrays, tail, deps=(), kernel=pack_kernel):
    width = sum(a.shape[-1] * (a.shape[0] if a.ndim == 3 else 1) for a in arrays) + tail.shape[1]
    height = arrays[0].shape[-2]
    return call(kernel, shape16(height, width), 0, height * width * 4, *arrays, tail, deps=deps)


def column_kernel(cuts, *refs):
    outs = refs[len(refs) - len(cuts) :]
    for k, ref in enumerate(refs[: len(refs) - len(cuts)]):
        for out, (first, last) in zip(outs, cuts):
            out[k] = ref[:, first:last]


def columns(shard, cuts, deps=()):
    size = lax.axis_size("dp")
    if size > FEW:
        pieces = lax.all_gather(shard, "dp")
        return [pieces[:, :, first:last] for first, last in cuts]
    near = [shard] + [flip(shard, "dp", mask) for mask in range(2, size, 2)]
    rows = shard.shape[0]
    return call(
        functools.partial(column_kernel, cuts),
        tuple(shape16(len(near), rows, last - first) for first, last in cuts),
        0,
        shard.size * 16,
        *near,
        deps=deps,
        name="columns",
    )


def beside_kernel(*refs):
    at = 0
    for ref in refs[:-1]:
        refs[-1][..., at : at + ref.shape[-1]] = ref[...]
        at += ref.shape[-1]


def beside(*arrays, deps=()):
    width = sum(a.shape[-1] for a in arrays)
    return call(beside_kernel, shape16(*arrays[0].shape[:-1], width), 0, arrays[0].size * 8, *arrays, deps=deps)


def core_stack_kernel(near, far, out):
    out[0] = near[:, out.shape[2] :]
    out[1] = far[:, out.shape[2] :]


def beside_stack(near, far):
    own, width = near.shape
    return call(core_stack_kernel, shape16(2, own, width // 2), 0, own * width * 4, near, far)


def lay_kernel(spans, bias_at, turned, me, near, other, *outs):
    count, rows = near.shape[:2]
    z, x = me[0] // 2, me[0] % 2
    total = None
    for m in range(count):
        slot = 2 * jnp.bitwise_xor(z, m)
        for at, source in ((slot + x, near), (slot + 1 - x, other)):
            start = pl.multiple_of(at * rows, 16)
            first = 0
            for k, span in enumerate(spans):
                out = outs[-1] if turned and k == len(spans) - 1 else outs[k]
                out[pl.ds(start, rows), :] = source[m, :, first : first + span].astype(out.dtype)
                first += span
            if bias_at:
                row = wide(source[m, 0:PAD, first : first + HD])
                total = row if total is None else total + row
    if turned:
        outs[len(spans) - 1][...] = low(jnp.transpose(outs[-1][...]))
    if bias_at:
        out = outs[0]
        below = slice(2 * count * rows, 2 * count * rows + PAD)
        out[below, :] = jnp.zeros((PAD, out.shape[1]), out.dtype)
        for k, at in enumerate(bias_at):
            out[below, at * HD : (at + 1) * HD] = low(jnp.broadcast_to(total[k : k + 1, :], (PAD, HD)))


def lay(near, spans, bias_at=(), turned=False, deps=()):
    size = lax.axis_size("dp")
    rows = near.shape[1]
    if size > FEW:
        whole = near.reshape(size * rows, -1)
        outs, first = [], 0
        for span in spans:
            outs.append(whole[:, first : first + span])
            first += span
        if turned:
            outs[-1] = outs[-1].T
        if bias_at:
            total = jnp.sum(wide(near[:, :, first : first + HD]), axis=0)[: len(bias_at)]
            total = jnp.zeros((spans[0] // HD, HD), jnp.float32).at[jnp.array(bias_at)].set(total)
            outs[0] = jnp.concatenate([outs[0], low(jnp.broadcast_to(total.reshape(1, -1), (PAD, spans[0])))], axis=0)
        return outs
    other = flip(near, "dp", 1)
    shapes = [shape16(size * rows, span) for span in spans]
    if turned:
        shapes[-1] = shape16(spans[-1], size * rows)
    if bias_at:
        shapes[0] = shape16(size * rows + PAD, spans[0])
    return call(
        functools.partial(lay_kernel, spans, bias_at, turned),
        tuple(shapes),
        0,
        near.size * 8,
        near,
        other,
        scalar=lax.axis_index("dp"),
        deps=deps,
        scratch=[pltpu.VMEM((size * rows, spans[-1]), jnp.float32)] if turned else [],
        name="lay",
    )


def spread(bias, rows):
    dp = lax.axis_size("dp")
    mine = lax.broadcasted_iota(jnp.int32, (1, dp, 1), 1) == lax.axis_index("dp")
    shard = bias.reshape(-1, 1, bias.shape[-1])
    placed = jnp.where(mine, shard, jnp.zeros((), bias.dtype)).reshape(shard.shape[0], HD)
    return jnp.concatenate([placed, jnp.zeros((rows - placed.shape[0], HD), bias.dtype)], axis=0)


def one_document(row_total, block_a, block_b):
    first, last = EDGE // BLK, (row_total - EDGE) // BLK
    return first <= block_a < last and first <= block_b < last


def project_kernel(normed, weights, out):
    heads = out.shape[0] // 3
    width = heads * HD
    depth = normed.shape[1]
    part = low(dot32(normed[...], weights[:depth, :], NN) + wide(weights[depth : depth + PAD, :])[0:1, :])
    for h in range(heads):
        for k in range(3):
            one = part[:, (h * 3 + k) * HD : (h * 3 + k + 1) * HD]
            out[k * heads + h] = one if k else low(wide(one) * HD ** -0.5)


def project(normed, weights):
    rows, depth = normed.shape
    count = weights.shape[1] // HD
    return pl.pallas_call(
        project_kernel,
        grid=(4,),
        in_specs=[
            pl.BlockSpec((rows // 4, depth), lambda i: (i, 0)),
            pl.BlockSpec(weights.shape, lambda i: (0, 0)),
        ],
        out_specs=pl.BlockSpec((count, rows // 4, HD), lambda i: (0, i, 0)),
        out_shape=shape16(count, rows, HD),
        compiler_params=ROOM,
        cost_estimate=cost(2 * rows * depth * count * HD, rows * depth * 6),
        name="project",
    )(normed, weights)


def attend_kernel(count, query_ref, key_ref, value_ref, seg_col, seg_row, *refs):
    out, lse, c_s = refs[count], refs[count + 1], refs[count + 2]
    rows = out.shape[0]
    c_s[...] = jnp.broadcast_to(seg_col[...], (rows, 128))
    for i in range(rows // BLK):
        mine = pl.ds(i * BLK, BLK)
        query = query_ref[0, mine, :]
        seg_mine = c_s[mine, :]
        seg_mine = jnp.concatenate([seg_mine, seg_mine], axis=1)
        tiles = []
        for j in range(i + 1):
            other = pl.ds(j * BLK, BLK)
            score = dot32(query, key_ref[0, other, :], NT)
            allowed = None
            if not one_document(rows, i, j):
                allowed = seg_mine == seg_row[:, other]
            if i == j:
                causal = lax.broadcasted_iota(jnp.int32, (BLK, BLK), 1) <= lax.broadcasted_iota(
                    jnp.int32, (BLK, BLK), 0
                )
                allowed = causal if allowed is None else allowed & causal
            if allowed is not None:
                score = jnp.where(allowed, score, -1e30)
            tiles.append(score)
        top = tiles[0]
        for tile in tiles[1:]:
            top = jnp.maximum(top, tile)
        top = jnp.max(top, axis=1, keepdims=True)
        total = None
        mixed = None
        for j, tile in enumerate(tiles):
            weight = jnp.exp(tile - top)
            total = weight if total is None else total + weight
            term = dot32(low(weight), value_ref[0, pl.ds(j * BLK, BLK), :], NN)
            mixed = term if mixed is None else mixed + term
        total = jnp.sum(total, axis=1, keepdims=True)
        out[mine, :] = low(mixed / total)
        log_total = jnp.broadcast_to(top + jnp.log(total), (BLK, 128))
        lse[:, mine] = jnp.transpose(log_total)[0:8, :]


def head_specs(split, head, count):
    rows = split.shape[1]
    return [
        pl.BlockSpec((1, rows, HD), lambda i, k=k: (k * count + head, 0, 0)) for k in range(3)
    ]


def full_spec(array):
    return pl.BlockSpec(array.shape, lambda i: (0,) * array.ndim)


def attend(split, head, seg_col, seg_row, deps=()):
    count, rows = split.shape[0] // 3, split.shape[1]
    return pl.pallas_call(
        functools.partial(attend_kernel, len(deps)),
        grid=(1,),
        in_specs=head_specs(split, head, count) + [full_spec(seg_col), full_spec(seg_row)] + [ANYWHERE] * len(deps),
        out_specs=[pl.BlockSpec((rows, HD), lambda i: (0, 0)), pl.BlockSpec((8, rows), lambda i: (0, 0))],
        out_shape=(shape16(rows, HD), shape32(8, rows)),
        scratch_shapes=[pltpu.VMEM((rows, 128), jnp.int32)],
        compiler_params=ROOM,
        cost_estimate=cost(7e9, rows * 1024, rows * rows // 2),
        name="attend",
    )(split, split, split, seg_col, seg_row, *deps)


def deal_kernel(me, *refs):
    heads, keep, chip, core = refs[:-3], refs[-3], refs[-2], refs[-1]
    own = keep.shape[0]
    for m, out in ((0, keep), (2, chip), (1, core.at[0]), (3, core.at[1])):
        start = pl.multiple_of(jnp.bitwise_xor(me[0], m) * own, own)
        for h, head in enumerate(heads):
            out[:, h * HD : (h + 1) * HD] = head[pl.ds(start, own), :]


def attend_back_kernel(
    head, count, extra, me, query_ref, key_ref, value_ref, mixed, near, core, far, lse, seg_col, seg_row, *refs
):
    earlier, out = refs[:extra], refs[extra + count]
    g_s, d_s, dk_s, dv_s, c_s = refs[extra + count + 1 :]
    rows = mixed.shape[0]
    own = rows // 4
    lanes = slice(head * HD, (head + 1) * HD)
    for m, piece in enumerate((near[:, lanes], core[0, :, lanes], far[:, lanes], core[1, :, lanes])):
        start = pl.multiple_of(jnp.bitwise_xor(me[0], m) * own, own)
        g_s[pl.ds(start, own), :] = piece
    c_s[...] = jnp.broadcast_to(seg_col[...], (rows, 128))
    inner = jnp.sum(wide(mixed[...]) * wide(g_s[...]), axis=1, keepdims=True)
    d_s[...] = jnp.transpose(jnp.broadcast_to(inner, (rows, 128)))[0:8, :]
    def store(kind, where, values):
        at = (3 * extra + kind) * HD
        out[where, at : at + HD] = values

    for i in range(rows // BLK):
        mine = pl.ds(i * BLK, BLK)
        query = query_ref[0, mine, :]
        grad_mine = g_s[mine, :]
        log_total = lse[0:1, mine]
        inner = d_s[0:1, mine]
        query_grad = None
        for j in range(i + 1):
            other = pl.ds(j * BLK, BLK)
            key = key_ref[0, other, :]
            score = dot32(key, query, NT)
            weight = jnp.exp(score - log_total)
            allowed = None
            if not one_document(rows, i, j):
                seg_other = c_s[other, :]
                seg_other = jnp.concatenate([seg_other, seg_other], axis=1)
                allowed = seg_other == seg_row[:, mine]
            if i == j:
                causal = lax.broadcasted_iota(jnp.int32, (BLK, BLK), 0) <= lax.broadcasted_iota(
                    jnp.int32, (BLK, BLK), 1
                )
                allowed = causal if allowed is None else allowed & causal
            if allowed is not None:
                weight = jnp.where(allowed, weight, 0.0)
            weight_grad = dot32(value_ref[0, other, :], grad_mine, NT)
            score_grad = low(weight * (weight_grad - inner))
            value_term = dot32(low(weight), grad_mine, NN)
            key_term = dot32(score_grad, query, NN)
            query_term = dot32(score_grad, key, TN)
            query_grad = query_term if query_grad is None else query_grad + query_term
            if i == j:
                dv_s[other, :] = value_term
                dk_s[other, :] = key_term
            else:
                dv_s[other, :] += value_term
                dk_s[other, :] += key_term
        store(0, mine, low(query_grad * HD ** -0.5))
    store(1, slice(None), low(dk_s[...]))
    store(2, slice(None), low(dv_s[...]))
    for h, ref in enumerate(earlier):
        out[:, 3 * h * HD : 3 * (h + 1) * HD] = ref[...]


def attend_back(split, head, mixed, near, core, far, lse, seg_col, seg_row, earlier=(), deps=()):
    count, rows = split.shape[0] // 3, split.shape[1]
    full = pltpu.VMEM((rows, HD), jnp.float32)
    operands = [mixed, near, core, far, lse, seg_col, seg_row, *earlier]
    shape = shape16(rows, 3 * (len(earlier) + 1) * HD)
    return pl.pallas_call(
        functools.partial(attend_back_kernel, head, len(deps), len(earlier)),
        grid=(1,),
        in_specs=[SCALAR]
        + head_specs(split, head, count)
        + [full_spec(array) for array in operands]
        + [ANYWHERE] * len(deps),
        out_specs=full_spec(shape),
        out_shape=shape,
        scratch_shapes=[
            pltpu.VMEM((rows, HD), jnp.bfloat16),
            pltpu.VMEM((8, rows), jnp.float32),
            full,
            full,
            pltpu.VMEM((rows, 128), jnp.int32),
        ],
        compiler_params=ROOM,
        cost_estimate=cost(15e9, rows * 2048, rows * rows // 2),
        name="attend_back",
    )(lax.axis_index("tensor").reshape(1), split, split, split, *operands, *deps)


def join_kernel(near, core, far, mine, other, tokens, bias, gain, shift, hidden, second, weights):
    span = near.shape[1]
    for k, piece in enumerate((mine[:span, :], other[:span, :], mine[span:, :], other[span:, :])):
        weights[k * span : (k + 1) * span, :] = piece
    branch = (
        dot32(near[...], weights[:span, :], NN)
        + dot32(core[0], weights[span : 2 * span, :], NN)
        + dot32(far[...], weights[2 * span :, :], NN)
    )
    total = wide(tokens[...]) + (branch + wide(bias[...]))
    hidden[...] = total
    normed, _ = normalized(total)
    second[...] = low(normed * gain[...] + shift[...])


def join(near, core, far, mine, other, tokens, bias, gain, shift, deps):
    own, width = tokens.shape
    return call(
        join_kernel,
        (shape32(own, width), shape16(own, width), shape16(2 * mine.shape[0], width)),
        2 * own * width * width,
        own * width * 12,
        near,
        core,
        far,
        mine,
        other,
        tokens,
        bias[None],
        gain[None],
        shift[None],
        deps=deps,
    )


def mlp_kernel(mine, other, top_a, top_b, up_a, up_b, down, active, pre_grads, own_part, core_part, bias_sum):
    depth, hidden = down.shape[0], up_a.shape[1]

    @pl.when(pl.program_id(0) == 0)
    def _():
        bias_sum[...] = jnp.zeros_like(bias_sum)

    for k, (source, top) in enumerate(((mine, top_a), (other, top_b))):
        rows = source[...]
        grad = top[...]
        part = None
        for half, up in enumerate((up_a, up_b)):
            lanes = slice(half * hidden, (half + 1) * hidden)
            pre = dot32(rows, up[:depth, :], NN) + wide(up[depth : depth + PAD, :])[0:1, :]
            act_grad = dot32(grad, down[:, lanes], NN)
            square = pre * pre
            bend = jnp.tanh(pre * (GELU_COEF + (GELU_COEF * 0.044715) * square))
            above = 0.5 + 0.5 * bend
            active[k, :, lanes] = low(pre * above)
            slope = above + (pre * (0.5 - 0.5 * bend * bend)) * (
                GELU_COEF + (3.0 * GELU_COEF * 0.044715) * square
            )
            pre_grad = low(act_grad * slope)
            pre_grads[k, :, lanes] = pre_grad
            bias_sum[0:1, lanes] += jnp.sum(wide(pre_grad), axis=0, keepdims=True)
            term = dot32(pre_grad, up[:depth, :], NT)
            part = term if part is None else part + term
        if k == 0:
            own_part[...] = part
        else:
            core_part[...] = low(part)


def mlp(mine, other, top_a, top_b, up_a, up_b, down):
    own, width = mine.shape
    hidden = up_a.shape[1]
    steps = 2
    rows = own // steps

    def whole(array):
        return pl.BlockSpec(array.shape, lambda i: (0,) * array.ndim)

    row_spec = pl.BlockSpec((rows, width), lambda i: (i, 0))
    wide_spec = pl.BlockSpec((2, rows, 2 * hidden), lambda i: (0, i, 0))
    return pl.pallas_call(
        mlp_kernel,
        grid=(steps,),
        in_specs=[row_spec] * 4 + [whole(array) for array in (up_a, up_b, down)],
        out_specs=[wide_spec, wide_spec, row_spec, row_spec, pl.BlockSpec((8, 2 * hidden), lambda i: (0, 0))],
        out_shape=(
            shape16(2, own, 2 * hidden),
            shape16(2, own, 2 * hidden),
            shape32(own, width),
            shape16(own, width),
            shape32(8, 2 * hidden),
        ),
        compiler_params=ROOM,
        cost_estimate=cost(12 * 2 * own * width * hidden, own * hidden * 12 + width * hidden * 8, 4 * own * hidden),
        name="mlp",
    )(mine, other, top_a, top_b, up_a, up_b, down)


def turn_kernel(mine, other, hidden, cotangent, weights, gain, a, b, hidden_grad, grad_attn, near, far, sums, c, d):
    half = weights.shape[0] // 2
    second_grad = mine[...] + wide(other[...])
    normed, scale = normalized(hidden[...])
    top = wide(cotangent[...])
    total = top + norm_back(normed, scale, second_grad * gain[...])
    hidden_grad[...] = total
    grad = low(total)
    grad_attn[...] = grad
    near[...] = low(dot32(grad, weights[:half, :], NT))
    far[...] = low(dot32(grad, weights[half:, :], NT))
    sums[0:1, :] = jnp.sum(wide(grad), axis=0, keepdims=True)
    sums[1:2, :] = jnp.sum(second_grad * normed, axis=0, keepdims=True)
    sums[2:3, :] = jnp.sum(second_grad, axis=0, keepdims=True)
    sums[3:4, :] = jnp.sum(top, axis=0, keepdims=True)


def turn(mine, other, hidden, cotangent, weights, gain, through):
    own, width = mine.shape
    half = weights.shape[0] // 2
    operands = (mine, other, hidden, cotangent, weights, gain[None])
    outs = (mine, other, shape16(own, half), shape16(own, half), shape32(4, width))
    return pl.pallas_call(
        turn_kernel,
        grid=(1,),
        in_specs=[full_spec(array) for array in operands] + [ANYWHERE] * 2,
        out_specs=[full_spec(array) for array in outs] + [ANYWHERE] * 2,
        out_shape=(
            shape32(own, width),
            shape16(own, width),
            shape16(own, half),
            shape16(own, half),
            shape32(4, width),
            *(jax.ShapeDtypeStruct(t.shape, t.dtype) for t in through),
        ),
        input_output_aliases={6: 5, 7: 6},
        compiler_params=ROOM,
        cost_estimate=cost(2 * own * width * width, own * width * 20),
        name="turn",
    )(*operands, *through)


def head_part(me, mask, own, first, last, weights):
    start = pl.multiple_of(jnp.bitwise_xor(me[0], mask) * own, own)
    cut = first.shape[1]
    depth = weights.shape[0] - PAD
    return dot32(first[pl.ds(start, own), :], weights[:depth, :cut], NT) + dot32(
        last[pl.ds(start, own), :], weights[:depth, cut:], NT
    )


def far_kernel(me, first, last, weights, chip, diagonal):
    own = chip.shape[0]
    diagonal[...] = low(head_part(me, 3, own, first, last, weights))
    chip[...] = head_part(me, 2, own, first, last, weights)


def near_kernel(me, first, last, weights, chip, diagonal, t0, t1, t2, t3, mine, core, sums, bias_sum):
    own = chip.shape[0]
    gain_sum, shift_sum = 0.0, 0.0
    for m, normed in enumerate((t0, t1, t2, t3)):
        if m < 2:
            part = head_part(me, m, own, first, last, weights)
            out = core if m else mine
            out[...] = part.astype(out.dtype)
        else:
            part = wide((diagonal if m == 3 else chip)[...])
        gain_sum = gain_sum + jnp.sum(part * wide(normed[...]), axis=0, keepdims=True)
        shift_sum = shift_sum + jnp.sum(part, axis=0, keepdims=True)
    sums[0:1, :] = gain_sum
    sums[1:2, :] = shift_sum
    heads = bias_sum.shape[1] // HD
    for source, base in ((first, 0), (last, heads - 1)):
        total = jnp.sum(wide(source[...]), axis=0, keepdims=True)
        for h in range(source.shape[1] // (3 * HD)):
            for row, kind in ((0, 0), (1, 2)):
                at = (3 * h + kind) * HD
                bias_sum[row : row + 1, (base + h) * HD : (base + h + 1) * HD] = total[:, at : at + HD]


def finish_kernel(first, last, out):
    heads = out.shape[2] // HD
    for source, base in ((first, 0), (last, heads - 1)):
        total = wide(source[0])
        for k in range(1, source.shape[0]):
            total = total + wide(source[k])
        for h in range(source.shape[2] // (3 * HD)):
            for kind in range(3):
                at = (3 * h + kind) * HD
                out[kind, :, (base + h) * HD : (base + h + 1) * HD] = total[:, at : at + HD]


def last_kernel(mine, core, chip, tokens, hidden_grad, gain, out):
    normed, scale = normalized(wide(tokens[...]))
    grad = (mine[...] + wide(core[...]) + wide(chip[...])) * gain[...]
    out[...] = hidden_grad[...] + norm_back(normed, scale, grad)


def call(kernel, out_shape, flops, size, *operands, scalar=None, deps=(), scratch=(), name=None):
    specs = [full_spec(array) for array in operands] + [ANYWHERE] * len(deps)
    outs = tuple(full_spec(shape) for shape in out_shape) if isinstance(out_shape, tuple) else full_spec(out_shape)
    count = len(operands)
    if scalar is not None:
        specs = [SCALAR] + specs
        operands = (scalar.reshape(1),) + operands
        count += 1
    skip = len(deps)

    def body(*refs):
        kernel(*refs[:count], *refs[count + skip :])

    return pl.pallas_call(
        body,
        grid=(1,),
        out_shape=out_shape,
        in_specs=specs,
        out_specs=outs,
        scratch_shapes=scratch,
        compiler_params=ROOM,
        cost_estimate=cost(flops, size),
        name=name or kernel.__name__,
    )(*operands, *deps)


def turned_rows_kernel(left, right, out):
    out[...] = low(jnp.transpose(dot32(right[...], left[...], TN)))


def gate_kernel(*refs):
    pass


def gate(values, *deps):
    return pl.pallas_call(
        gate_kernel,
        in_specs=[ANYWHERE] * (1 + len(deps)),
        out_specs=ANYWHERE,
        out_shape=jax.ShapeDtypeStruct(values.shape, values.dtype),
        input_output_aliases={0: 0},
        name="gate",
    )(values, *deps)


def plain(values):
    return with_layout_constraint(values, Layout(major_to_minor=tuple(range(values.ndim))))


def flip(values, axis, mask):
    size = lax.axis_size(axis)
    return plain(lax.ppermute(plain(values), axis, [(i, i ^ mask) for i in range(size)]))


def core_swap(values):
    return flip(values, "tensor", 1)


def chip_swap(values):
    return flip(values, "tensor", 2)


def place(buffer, piece, index):
    return lax.dynamic_update_slice_in_dim(buffer, piece[None], index, 0)


def pick(blocks, index):
    return lax.dynamic_index_in_dim(blocks, index, 0, keepdims=False)


def swap_blocks(whole):
    blocks = low(whole).reshape((lax.axis_size("dp"), -1) + whole.shape[1:])
    return lax.all_to_all(plain(blocks), "dp", 0, 0, tiled=True)


def halves(whole):
    size = lax.axis_size("dp")
    me = lax.axis_index("dp")
    blocks = whole.reshape((size // 2, 2, -1) + whole.shape[1:])
    keep = lax.dynamic_index_in_dim(blocks, me % 2, 1, keepdims=False)
    return keep, low(lax.dynamic_index_in_dim(blocks, 1 - me % 2, 1, keepdims=False))


def sum_column(column, sent):
    size = lax.axis_size("dp")
    me = lax.axis_index("dp")
    total = pick(column, me // 2)
    for mask in range(2, size, 2):
        total = total + wide(flip(pick(sent, (me ^ mask) // 2), "dp", mask))
    return total


def sum_everywhere(values):
    for mask in (1, 2):
        values = values + flip(values, "tensor", mask)
    mask = 1
    while mask < lax.axis_size("dp"):
        values = values + flip(values, "dp", mask)
        mask *= 2
    return values


def contract_rows(left_mat, right_mat):
    return dot32(left_mat, right_mat, TN)


def on_device(
    tokens,
    segment,
    cotangent,
    ln1_gain,
    ln1_bias,
    w_qkv,
    qv_bias,
    w_out,
    out_bias,
    ln2_gain,
    ln2_bias,
    w_up,
    up_bias,
    w_down,
    down_bias,
):
    dp = lax.axis_size("dp")
    place_dp = lax.axis_index("dp")
    me = lax.axis_index("tensor")
    own, width = tokens.shape
    rows_shard = w_qkv.shape[1]
    span = w_qkv.shape[2]
    hidden = w_up.shape[1]

    heads = span // HD

    out_turned = w_out.T
    out_turned_chip = chip_swap(out_turned)
    qkv_pack = pack([w_qkv], spread(qv_bias, PAD), kernel=pack_heads_kernel)
    from_core = core_swap(tokens)
    from_chip = chip_swap(tokens)
    top_core = core_swap(cotangent)
    first_norm, normed_own = first_norm_of(tokens, ln1_gain, ln1_bias, me, qkv_pack)
    first_norm, normed_core = first_norm_of(from_core, ln1_gain, ln1_bias, me ^ 1, normed_own, first_norm)
    (qkv_column,) = columns(qkv_pack, ((0, 3 * span + HD),), (normed_core,))
    from_chip = gate(from_chip, qkv_column)
    from_diagonal = core_swap(from_chip)

    edge = hidden + 2 * span + HD
    rest_pack = pack(
        [w_down.T, w_up, out_turned, out_turned_chip], spread(up_bias, PAD), deps=(qkv_column, top_core)
    )
    bias_at = tuple(3 * h + kind for kind in (0, 2) for h in range(heads))
    (qkv_full,) = lay(qkv_column, (3 * span,), bias_at, deps=(rest_pack,))
    first_norm, normed_chip = first_norm_of(from_chip, ln1_gain, ln1_bias, me ^ 2, qkv_full, first_norm)
    first_norm, normed_diagonal = first_norm_of(from_diagonal, ln1_gain, ln1_bias, me ^ 3, normed_chip, first_norm)
    first_norm = first_norm.reshape(4 * own, width)

    seg_col, seg_row = segment[:, None], segment[None, :]
    split = project(first_norm, qkv_full)
    heads_out, log_totals = [], []
    for head in range(heads):
        deps = () if head == 0 else (up_column, heads_out[-1])
        out, log_total = attend(split, head, seg_col, seg_row, deps)
        heads_out.append(out)
        log_totals.append(log_total)
        if head == 0:
            down_column, up_column = columns(rest_pack, ((0, hidden), (hidden, hidden + edge)), (out,))

    mixed_own, mixed_chip, to_core = call(
        deal_kernel,
        (shape16(own, span), shape16(own, span), shape16(2, own, span)),
        0,
        own * span * 24,
        *heads_out,
        scalar=me,
    )
    mixed_core = core_swap(to_core)
    down_columns = beside(down_column, chip_swap(down_column), deps=(to_core,))
    up_own, out_pair = lay(up_column, (hidden, 2 * span), tuple(range(hidden // HD)), True, (down_columns,))
    mixed_far = beside(mixed_chip, mixed_core[1], deps=(up_own,))
    mixed_far = chip_swap(mixed_far)
    up_own = gate(up_own, mixed_far)
    out_core = core_swap(out_pair)
    hidden_one, second, out_full = join(
        mixed_own, mixed_core, mixed_far, out_pair, out_core, tokens, out_bias, ln2_gain, ln2_bias, (up_own,)
    )
    (down_pair,) = lay(down_columns, (2 * hidden,), deps=(second,))

    up_chip = gate(chip_swap(up_own), down_pair)
    second_core = gate(core_swap(second), up_chip)
    active, pre_grad, second_own, second_far, up_bias_sum = mlp(
        second, second_core, cotangent, top_core, up_own, up_chip, down_pair
    )

    few = lax.axis_size("dp") <= FEW
    hidden_grad, grad_attn, grad_near, grad_far, turn_sums, active, pre_grad = turn(
        second_own, core_swap(second_far), hidden_one, cotangent, out_full, ln2_gain, (active, pre_grad)
    )
    down_whole = contract_rows(cotangent, active[0]) + contract_rows(top_core, active[1])
    down_keep, down_give = halves(down_whole) if few else (None, low(down_whole))
    grad_far = chip_swap(grad_far)
    grad_core = core_swap(beside_stack(grad_near, grad_far))

    up_whole = contract_rows(second, pre_grad[0]) + contract_rows(second_core, pre_grad[1])
    up_chip_grad = chip_swap(gate(low(up_whole[:, hidden:]), grad_far))

    out_part_near = contract_rows(beside(mixed_own, mixed_core[0]), grad_attn)
    out_part_far = contract_rows(mixed_far, grad_attn)
    out_core_grad = core_swap(low(jnp.stack([out_part_near[span:], out_part_far[span:]])))
    out_mid = low(out_part_far[:span] + wide(out_core_grad[1]))
    out_grad = out_part_near[:span] + wide(out_core_grad[0]) + wide(chip_swap(out_mid))
    up_out_whole = jnp.concatenate([up_whole[:, :hidden] + wide(up_chip_grad), out_grad.T], axis=1)

    def back(head, earlier, deps):
        return attend_back(
            split,
            head,
            heads_out[head],
            grad_near,
            grad_core,
            grad_far,
            log_totals[head],
            seg_col,
            seg_row,
            earlier,
            deps,
        )

    grads = [back(0, (), (out_mid,))]
    if few:
        down_column = wide(down_keep) + wide(gate(flip(down_give, "dp", 1), grads[0]))
        down_sent = low(down_column)
        up_keep, up_give = halves(up_out_whole)
    for head in range(1, heads):
        last = head == heads - 1
        deps = tuple(grads[-1:]) if last else (down_sent,) if few else ()
        if last:
            first_whole = low(contract_rows(first_norm, grads[-1]))
            deps += (first_whole, up_give) if few else (first_whole,)
        grads.append(back(head, () if last else tuple(grads), deps))
    first_heads, last_head = grads[-2:]
    first_blocks = swap_blocks(first_whole)
    if few:
        up_column = wide(up_keep) + wide(flip(up_give, "dp", 1))
        up_sent = low(up_column)
        down_part = sum_column(down_column, down_sent)
    else:
        down_part = jnp.sum(wide(swap_blocks(down_give)), axis=0)
        up_sent = swap_blocks(up_out_whole)

    far_size = own * width * 8
    part_chip, part_diagonal = call(
        far_kernel,
        (shape32(own, width), shape16(own, width)),
        own * width * span * 12,
        far_size,
        first_heads,
        last_head,
        qkv_full,
        scalar=me,
    )
    from_diagonal = gate(core_swap(part_diagonal), up_sent, down_part, first_blocks)
    chip_sum = low(part_chip + wide(from_diagonal))
    last_whole = call(turned_rows_kernel, shape16(width, 3 * HD), 0, own * width * 8, first_norm, last_head)
    part_own, part_core, first_sums, bias_sum = call(
        near_kernel,
        (shape32(own, width), shape16(own, width), shape32(2, width), shape32(2, span)),
        own * width * span * 12,
        far_size * 2,
        first_heads,
        last_head,
        qkv_full,
        part_chip,
        part_diagonal,
        normed_own,
        normed_core,
        normed_chip,
        normed_diagonal,
        scalar=me,
        deps=(chip_sum, last_whole),
    )
    chip_sum = chip_swap(chip_sum)
    (w_qkv_grad_out,) = call(
        finish_kernel, (shape32(3, rows_shard, span),), 0, width * span * 6, first_blocks, swap_blocks(last_whole)
    )

    up_out = sum_column(up_column, up_sent) if few else jnp.sum(wide(up_sent), axis=0)
    down_grad_out = (down_part[:, :hidden] + wide(chip_swap(low(down_part[:, hidden:])))).T
    up_grad_out = up_out[:, :hidden]
    w_out_grad_out = up_out[:, hidden:].T

    active = gate(active.reshape(2 * own, 2 * hidden), part_own)
    mlp_part = dot32(active, down_pair, NT)
    mlp_branch = mlp_part[:own] + wide(core_swap(low(mlp_part[own:])))
    block_out = hidden_one + (mlp_branch + wide(down_bias))

    (token_grad,) = call(
        last_kernel,
        (shape32(own, width),),
        own * width * 30,
        own * width * 16,
        part_own,
        core_swap(part_core),
        chip_sum,
        tokens,
        hidden_grad,
        ln1_gain[None],
    )

    bias_spread = jnp.zeros((4, 2, span), jnp.float32)
    bias_spread = place(bias_spread, bias_sum, me)
    up_rows = jnp.zeros((4, hidden), jnp.float32)
    up_rows = place(up_rows, up_bias_sum[0, :hidden], me)
    up_rows = place(up_rows, up_bias_sum[0, hidden:], me ^ 2)
    sums = sum_everywhere(
        jnp.concatenate([first_sums, turn_sums, bias_spread.reshape(-1, width), up_rows.reshape(-1, width)], axis=0)
    )
    count = bias_spread.size // width
    qv_bias_grad = pick(sums[6 : 6 + count].reshape((4, 2, span // HD, dp, qv_bias.shape[2])), me)
    qv_bias_grad = lax.dynamic_index_in_dim(qv_bias_grad, place_dp, 2, keepdims=False)
    up_bias_grad = pick(sums[6 + count :].reshape((4, hidden // HD, dp, up_bias.shape[1])), me)
    up_bias_grad = lax.dynamic_index_in_dim(up_bias_grad, place_dp, 1, keepdims=False)
    return (
        block_out,
        token_grad,
        sums[0],
        sums[1],
        w_qkv_grad_out,
        qv_bias_grad,
        w_out_grad_out,
        sums[2],
        sums[3],
        sums[4],
        up_grad_out,
        up_bias_grad,
        down_grad_out,
        sums[5],
    )


def solution(mesh):
    in_specs = (
        P(("dp", "tensor"), None),
        P("dp"),
        P(("dp", "tensor"), None),
        P(),
        P(),
        P(None, "dp", "tensor"),
        P(None, "tensor", "dp"),
        P("tensor", "dp"),
        P(),
        P(),
        P(),
        P("dp", "tensor"),
        P("tensor", "dp"),
        P("tensor", "dp"),
        P(),
    )
    out_specs = (
        P(("dp", "tensor"), None),
        P(("dp", "tensor"), None),
        P(),
        P(),
        P(None, "dp", "tensor"),
        P(None, "tensor", "dp"),
        P("tensor", "dp"),
        P(),
        P(),
        P(),
        P("dp", "tensor"),
        P("tensor", "dp"),
        P("tensor", "dp"),
        P(),
    )
    return jax.shard_map(
        on_device, mesh=mesh, in_specs=in_specs, out_specs=out_specs, check_vma=False
    )
```

```python
import functools

import jax
import jax.numpy as jnp
from jax import lax
from jax.experimental import pallas as pl
from jax.experimental.layout import Layout, with_layout_constraint
from jax.experimental.pallas import tpu as pltpu
from jax.sharding import PartitionSpec as P

HD = 64
BLK = 256
EDGE = 512
FEW = 8
PAD = 16
EPSILON = 1e-05
GELU_COEF = 0.7978845608028654
NT = (((1,), (1,)), ((), ()))
TN = (((0,), (0,)), ((), ()))
NN = (((1,), (0,)), ((), ()))
ROOM = pltpu.CompilerParams(vmem_limit_bytes=48 * 2**20)
SCALAR = pl.BlockSpec(memory_space=pltpu.SMEM)
ANYWHERE = pl.BlockSpec(memory_space=pl.ANY)


def low(values):
    return values.astype(jnp.bfloat16)


def wide(values):
    return values.astype(jnp.float32)


def shape16(*dims):
    return jax.ShapeDtypeStruct(dims, jnp.bfloat16)


def shape32(*dims):
    return jax.ShapeDtypeStruct(dims, jnp.float32)


def cost(flops, size, exps=0):
    return pl.CostEstimate(flops=1, bytes_accessed=1, transcendentals=0)


def dot32(left, right, dims):
    return lax.dot_general(left, right, dims, preferred_element_type=jnp.float32)


def normalized(values_in):
    row_mean = jnp.mean(values_in, axis=-1, keepdims=True)
    centered = values_in - row_mean
    variance = jnp.mean(centered * centered, axis=-1, keepdims=True)
    scale = lax.rsqrt(variance + EPSILON)
    return centered * scale, scale


def norm_back(normed, scale, grad):
    mean_grad = jnp.mean(grad, axis=-1, keepdims=True)
    mean_both = jnp.mean(grad * normed, axis=-1, keepdims=True)
    return scale * (grad - mean_grad - normed * mean_both)


def first_kernel(index, piece, gain, shift, *rest):
    normed, _ = normalized(wide(piece[...]))
    rest[-2][0] = low(normed * gain[...] + shift[...])
    rest[-1][...] = low(normed)


def first_norm_of(piece, gain, shift, index, dep, buffer=None):
    own, width = piece.shape
    steps = 2
    rows = own // steps
    row_spec = pl.BlockSpec((1, width), lambda i, at: (0, 0))
    operands = [index.reshape(1), piece, gain[None], shift[None], dep]
    in_specs = [pl.BlockSpec((rows, width), lambda i, at: (i, 0)), row_spec, row_spec, ANYWHERE]
    aliases = {}
    if buffer is not None:
        operands.append(buffer)
        in_specs.append(ANYWHERE)
        aliases = {5: 0}
    return pl.pallas_call(
        first_kernel,
        grid_spec=pltpu.PrefetchScalarGridSpec(
            num_scalar_prefetch=1,
            grid=(steps,),
            in_specs=in_specs,
            out_specs=[
                pl.BlockSpec((1, rows, width), lambda i, at: (at[0], i, 0)),
                pl.BlockSpec((rows, width), lambda i, at: (i, 0)),
            ],
        ),
        out_shape=(shape16(4, own, width), shape16(own, width)),
        input_output_aliases=aliases,
        cost_estimate=cost(own * width * 12, own * width * 4),
        name="first_norm",
    )(*operands)


def pack_kernel(*refs):
    out = refs[-1]
    at = 0
    for ref in refs[:-2]:
        out[:, at : at + ref.shape[1]] = ref[...]
        at += ref.shape[1]
    out[:, at:] = jnp.zeros((out.shape[0], out.shape[1] - at), out.dtype)
    tail = refs[-2]
    count = min(tail.shape[0], out.shape[0])
    out[:count, at : at + tail.shape[1]] = tail[:count, :]


def pack_heads_kernel(weights, tail, out):
    kinds, height, span = weights.shape
    for h in range(span // HD):
        for k in range(kinds):
            at = (h * kinds + k) * HD
            out[:, at : at + HD] = weights[k, :, h * HD : (h + 1) * HD]
    out[:, kinds * span :] = jnp.zeros((height, tail.shape[1]), out.dtype)
    count = min(tail.shape[0], height)
    out[:count, kinds * span :] = tail[:count, :]


def pack(arrays, tail, deps=(), kernel=pack_kernel):
    width = sum(a.shape[-1] * (a.shape[0] if a.ndim == 3 else 1) for a in arrays) + tail.shape[1]
    height = arrays[0].shape[-2]
    return call(kernel, shape16(height, width), 0, height * width * 4, *arrays, tail, deps=deps)


def column_kernel(cuts, *refs):
    outs = refs[len(refs) - len(cuts) :]
    for k, ref in enumerate(refs[: len(refs) - len(cuts)]):
        for out, (first, last) in zip(outs, cuts):
            out[k] = ref[:, first:last]


def columns(shard, cuts, deps=()):
    size = lax.axis_size("dp")
    if size > FEW:
        pieces = lax.all_gather(shard, "dp")
        return [pieces[:, :, first:last] for first, last in cuts]
    near = [shard] + [flip(shard, "dp", mask) for mask in range(2, size, 2)]
    rows = shard.shape[0]
    return call(
        functools.partial(column_kernel, cuts),
        tuple(shape16(len(near), rows, last - first) for first, last in cuts),
        0,
        shard.size * 16,
        *near,
        deps=deps,
        name="columns",
    )


def beside_kernel(*refs):
    at = 0
    for ref in refs[:-1]:
        refs[-1][..., at : at + ref.shape[-1]] = ref[...]
        at += ref.shape[-1]


def beside(*arrays, deps=()):
    width = sum(a.shape[-1] for a in arrays)
    return call(beside_kernel, shape16(*arrays[0].shape[:-1], width), 0, arrays[0].size * 8, *arrays, deps=deps)


def core_stack_kernel(near, far, out):
    out[0] = near[:, out.shape[2] :]
    out[1] = far[:, out.shape[2] :]


def beside_stack(near, far):
    own, width = near.shape
    return call(core_stack_kernel, shape16(2, own, width // 2), 0, own * width * 4, near, far)


def lay_kernel(spans, bias_at, turned, me, near, other, *outs):
    count, rows = near.shape[:2]
    z, x = me[0] // 2, me[0] % 2
    total = None
    for m in range(count):
        slot = 2 * jnp.bitwise_xor(z, m)
        for at, source in ((slot + x, near), (slot + 1 - x, other)):
            start = pl.multiple_of(at * rows, 16)
            first = 0
            for k, span in enumerate(spans):
                out = outs[-1] if turned and k == len(spans) - 1 else outs[k]
                out[pl.ds(start, rows), :] = source[m, :, first : first + span].astype(out.dtype)
                first += span
            if bias_at:
                row = wide(source[m, 0:PAD, first : first + HD])
                total = row if total is None else total + row
    if turned:
        outs[len(spans) - 1][...] = low(jnp.transpose(outs[-1][...]))
    if bias_at:
        out = outs[0]
        below = slice(2 * count * rows, 2 * count * rows + PAD)
        out[below, :] = jnp.zeros((PAD, out.shape[1]), out.dtype)
        for k, at in enumerate(bias_at):
            out[below, at * HD : (at + 1) * HD] = low(jnp.broadcast_to(total[k : k + 1, :], (PAD, HD)))


def lay(near, spans, bias_at=(), turned=False, deps=()):
    size = lax.axis_size("dp")
    rows = near.shape[1]
    if size > FEW:
        whole = near.reshape(size * rows, -1)
        outs, first = [], 0
        for span in spans:
            outs.append(whole[:, first : first + span])
            first += span
        if turned:
            outs[-1] = outs[-1].T
        if bias_at:
            total = jnp.sum(wide(near[:, :, first : first + HD]), axis=0)[: len(bias_at)]
            total = jnp.zeros((spans[0] // HD, HD), jnp.float32).at[jnp.array(bias_at)].set(total)
            outs[0] = jnp.concatenate([outs[0], low(jnp.broadcast_to(total.reshape(1, -1), (PAD, spans[0])))], axis=0)
        return outs
    other = flip(near, "dp", 1)
    shapes = [shape16(size * rows, span) for span in spans]
    if turned:
        shapes[-1] = shape16(spans[-1], size * rows)
    if bias_at:
        shapes[0] = shape16(size * rows + PAD, spans[0])
    return call(
        functools.partial(lay_kernel, spans, bias_at, turned),
        tuple(shapes),
        0,
        near.size * 8,
        near,
        other,
        scalar=lax.axis_index("dp"),
        deps=deps,
        scratch=[pltpu.VMEM((size * rows, spans[-1]), jnp.float32)] if turned else [],
        name="lay",
    )


def spread(bias, rows):
    dp = lax.axis_size("dp")
    mine = lax.broadcasted_iota(jnp.int32, (1, dp, 1), 1) == lax.axis_index("dp")
    shard = bias.reshape(-1, 1, bias.shape[-1])
    placed = jnp.where(mine, shard, jnp.zeros((), bias.dtype)).reshape(shard.shape[0], HD)
    return jnp.concatenate([placed, jnp.zeros((rows - placed.shape[0], HD), bias.dtype)], axis=0)


def one_document(row_total, block_a, block_b):
    first, last = EDGE // BLK, (row_total - EDGE) // BLK
    return first <= block_a < last and first <= block_b < last


def project_kernel(normed, weights, out):
    heads = out.shape[0] // 3
    width = heads * HD
    depth = normed.shape[1]
    part = low(dot32(normed[...], weights[:depth, :], NN) + wide(weights[depth : depth + PAD, :])[0:1, :])
    for h in range(heads):
        for k in range(3):
            one = part[:, (h * 3 + k) * HD : (h * 3 + k + 1) * HD]
            out[k * heads + h] = one if k else low(wide(one) * HD ** -0.5)


def project(normed, weights):
    rows, depth = normed.shape
    count = weights.shape[1] // HD
    return pl.pallas_call(
        project_kernel,
        grid=(4,),
        in_specs=[
            pl.BlockSpec((rows // 4, depth), lambda i: (i, 0)),
            pl.BlockSpec(weights.shape, lambda i: (0, 0)),
        ],
        out_specs=pl.BlockSpec((count, rows // 4, HD), lambda i: (0, i, 0)),
        out_shape=shape16(count, rows, HD),
        compiler_params=ROOM,
        cost_estimate=cost(2 * rows * depth * count * HD, rows * depth * 6),
        name="project",
    )(normed, weights)


def attend_kernel(count, query_ref, key_ref, value_ref, seg_row, *refs):
    out, lse, c_s = refs[count], refs[count + 1], refs[count + 2]
    rows = out.shape[0]
    c_s[...] = jnp.transpose(jnp.broadcast_to(seg_row[...], (128, rows)))
    for i in range(rows // BLK):
        mine = pl.ds(i * BLK, BLK)
        query = query_ref[0, mine, :]
        seg_mine = c_s[mine, :]
        seg_mine = jnp.concatenate([seg_mine, seg_mine], axis=1)
        tiles = []
        for j in range(i + 1):
            other = pl.ds(j * BLK, BLK)
            score = dot32(query, key_ref[0, other, :], NT)
            allowed = None
            if not one_document(rows, i, j):
                allowed = seg_mine == seg_row[:, other]
            if i == j:
                causal = lax.broadcasted_iota(jnp.int32, (BLK, BLK), 1) <= lax.broadcasted_iota(
                    jnp.int32, (BLK, BLK), 0
                )
                allowed = causal if allowed is None else allowed & causal
            if allowed is not None:
                score = jnp.where(allowed, score, -1e30)
            tiles.append(score)
        top = tiles[0]
        for tile in tiles[1:]:
            top = jnp.maximum(top, tile)
        top = jnp.max(top, axis=1, keepdims=True)
        total = None
        mixed = None
        for j, tile in enumerate(tiles):
            weight = jnp.exp(tile - top)
            total = weight if total is None else total + weight
            term = dot32(low(weight), value_ref[0, pl.ds(j * BLK, BLK), :], NN)
            mixed = term if mixed is None else mixed + term
        total = jnp.sum(total, axis=1, keepdims=True)
        out[mine, :] = low(mixed / total)
        log_total = jnp.broadcast_to(top + jnp.log(total), (BLK, 128))
        lse[:, mine] = jnp.transpose(log_total)[0:8, :]


def head_specs(split, head, count):
    rows = split.shape[1]
    return [
        pl.BlockSpec((1, rows, HD), lambda i, k=k: (k * count + head, 0, 0)) for k in range(3)
    ]


def full_spec(array):
    return pl.BlockSpec(array.shape, lambda i: (0,) * array.ndim)


def attend(split, head, seg_row, deps=()):
    count, rows = split.shape[0] // 3, split.shape[1]
    return pl.pallas_call(
        functools.partial(attend_kernel, len(deps)),
        grid=(1,),
        in_specs=head_specs(split, head, count) + [full_spec(seg_row)] + [ANYWHERE] * len(deps),
        out_specs=[pl.BlockSpec((rows, HD), lambda i: (0, 0)), pl.BlockSpec((8, rows), lambda i: (0, 0))],
        out_shape=(shape16(rows, HD), shape32(8, rows)),
        scratch_shapes=[pltpu.VMEM((rows, 128), jnp.int32)],
        compiler_params=ROOM,
        cost_estimate=cost(7e9, rows * 1024, rows * rows // 2),
        name="attend",
    )(split, split, split, seg_row, *deps)


def deal_kernel(me, *refs):
    heads, keep, chip, core = refs[:-3], refs[-3], refs[-2], refs[-1]
    own = keep.shape[0]
    for m, out in ((0, keep), (2, chip), (1, core.at[0]), (3, core.at[1])):
        start = pl.multiple_of(jnp.bitwise_xor(me[0], m) * own, own)
        for h, head in enumerate(heads):
            out[:, h * HD : (h + 1) * HD] = head[pl.ds(start, own), :]


def attend_back_kernel(
    head, count, extra, me, query_ref, key_ref, value_ref, mixed, near, core, far, lse, seg_row, *refs
):
    earlier, out = refs[:extra], refs[extra + count]
    g_s, d_s, dk_s, dv_s, c_s = refs[extra + count + 1 :]
    rows = mixed.shape[0]
    own = rows // 4
    lanes = slice(head * HD, (head + 1) * HD)
    for m, piece in enumerate((near[:, lanes], core[0, :, lanes], far[:, lanes], core[1, :, lanes])):
        start = pl.multiple_of(jnp.bitwise_xor(me[0], m) * own, own)
        g_s[pl.ds(start, own), :] = piece
    c_s[...] = jnp.transpose(jnp.broadcast_to(seg_row[...], (128, rows)))
    inner = jnp.sum(wide(mixed[...]) * wide(g_s[...]), axis=1, keepdims=True)
    d_s[...] = jnp.transpose(jnp.broadcast_to(inner, (rows, 128)))[0:8, :]
    def store(kind, where, values):
        at = (3 * extra + kind) * HD
        out[where, at : at + HD] = values

    for i in range(rows // BLK):
        mine = pl.ds(i * BLK, BLK)
        query = query_ref[0, mine, :]
        grad_mine = g_s[mine, :]
        log_total = lse[0:1, mine]
        inner = d_s[0:1, mine]
        query_grad = None
        for j in range(i + 1):
            other = pl.ds(j * BLK, BLK)
            key = key_ref[0, other, :]
            score = dot32(key, query, NT)
            weight = jnp.exp(score - log_total)
            allowed = None
            if not one_document(rows, i, j):
                seg_other = c_s[other, :]
                seg_other = jnp.concatenate([seg_other, seg_other], axis=1)
                allowed = seg_other == seg_row[:, mine]
            if i == j:
                causal = lax.broadcasted_iota(jnp.int32, (BLK, BLK), 0) <= lax.broadcasted_iota(
                    jnp.int32, (BLK, BLK), 1
                )
                allowed = causal if allowed is None else allowed & causal
            if allowed is not None:
                weight = jnp.where(allowed, weight, 0.0)
            weight_grad = dot32(value_ref[0, other, :], grad_mine, NT)
            score_grad = low(weight * (weight_grad - inner))
            value_term = dot32(low(weight), grad_mine, NN)
            key_term = dot32(score_grad, query, NN)
            query_term = dot32(score_grad, key, TN)
            query_grad = query_term if query_grad is None else query_grad + query_term
            if i == j:
                dv_s[other, :] = value_term
                dk_s[other, :] = key_term
            else:
                dv_s[other, :] += value_term
                dk_s[other, :] += key_term
        store(0, mine, low(query_grad * HD ** -0.5))
    store(1, slice(None), low(dk_s[...]))
    store(2, slice(None), low(dv_s[...]))
    for h, ref in enumerate(earlier):
        out[:, 3 * h * HD : 3 * (h + 1) * HD] = ref[...]


def attend_back(split, head, mixed, near, core, far, lse, seg_row, earlier=(), deps=()):
    count, rows = split.shape[0] // 3, split.shape[1]
    full = pltpu.VMEM((rows, HD), jnp.float32)
    operands = [mixed, near, core, far, lse, seg_row, *earlier]
    shape = shape16(rows, 3 * (len(earlier) + 1) * HD)
    return pl.pallas_call(
        functools.partial(attend_back_kernel, head, len(deps), len(earlier)),
        grid=(1,),
        in_specs=[SCALAR]
        + head_specs(split, head, count)
        + [full_spec(array) for array in operands]
        + [ANYWHERE] * len(deps),
        out_specs=full_spec(shape),
        out_shape=shape,
        scratch_shapes=[
            pltpu.VMEM((rows, HD), jnp.bfloat16),
            pltpu.VMEM((8, rows), jnp.float32),
            full,
            full,
            pltpu.VMEM((rows, 128), jnp.int32),
        ],
        compiler_params=ROOM,
        cost_estimate=cost(15e9, rows * 2048, rows * rows // 2),
        name="attend_back",
    )(lax.axis_index("tensor").reshape(1), split, split, split, *operands, *deps)


def join_kernel(near, core, far, mine, other, tokens, bias, gain, shift, hidden, second, weights):
    span = near.shape[1]
    for k, piece in enumerate((mine[:span, :], other[:span, :], mine[span:, :], other[span:, :])):
        weights[k * span : (k + 1) * span, :] = piece
    branch = (
        dot32(near[...], weights[:span, :], NN)
        + dot32(core[0], weights[span : 2 * span, :], NN)
        + dot32(far[...], weights[2 * span :, :], NN)
    )
    total = wide(tokens[...]) + (branch + wide(bias[...]))
    hidden[...] = total
    normed, _ = normalized(total)
    second[...] = low(normed * gain[...] + shift[...])


def join(near, core, far, mine, other, tokens, bias, gain, shift, deps):
    own, width = tokens.shape
    return call(
        join_kernel,
        (shape32(own, width), shape16(own, width), shape16(2 * mine.shape[0], width)),
        2 * own * width * width,
        own * width * 12,
        near,
        core,
        far,
        mine,
        other,
        tokens,
        bias[None],
        gain[None],
        shift[None],
        deps=deps,
    )


def mlp_kernel(mine, other, top_a, top_b, up_a, up_b, down, active, pre_grads, own_part, core_part, bias_sum):
    depth, hidden = down.shape[0], up_a.shape[1]

    @pl.when(pl.program_id(0) == 0)
    def _():
        bias_sum[...] = jnp.zeros_like(bias_sum)

    for k, (source, top) in enumerate(((mine, top_a), (other, top_b))):
        rows = source[...]
        grad = top[...]
        part = None
        for half, up in enumerate((up_a, up_b)):
            lanes = slice(half * hidden, (half + 1) * hidden)
            pre = dot32(rows, up[:depth, :], NN) + wide(up[depth : depth + PAD, :])[0:1, :]
            act_grad = dot32(grad, down[:, lanes], NN)
            square = pre * pre
            bend = jnp.tanh(pre * (GELU_COEF + (GELU_COEF * 0.044715) * square))
            above = 0.5 + 0.5 * bend
            active[k, :, lanes] = low(pre * above)
            slope = above + (pre * (0.5 - 0.5 * bend * bend)) * (
                GELU_COEF + (3.0 * GELU_COEF * 0.044715) * square
            )
            pre_grad = low(act_grad * slope)
            pre_grads[k, :, lanes] = pre_grad
            bias_sum[0:1, lanes] += jnp.sum(wide(pre_grad), axis=0, keepdims=True)
            term = dot32(pre_grad, up[:depth, :], NT)
            part = term if part is None else part + term
        if k == 0:
            own_part[...] = part
        else:
            core_part[...] = low(part)


def mlp(mine, other, top_a, top_b, up_a, up_b, down):
    own, width = mine.shape
    hidden = up_a.shape[1]
    steps = 2
    rows = own // steps

    def whole(array):
        return pl.BlockSpec(array.shape, lambda i: (0,) * array.ndim)

    row_spec = pl.BlockSpec((rows, width), lambda i: (i, 0))
    wide_spec = pl.BlockSpec((2, rows, 2 * hidden), lambda i: (0, i, 0))
    return pl.pallas_call(
        mlp_kernel,
        grid=(steps,),
        in_specs=[row_spec] * 4 + [whole(array) for array in (up_a, up_b, down)],
        out_specs=[wide_spec, wide_spec, row_spec, row_spec, pl.BlockSpec((8, 2 * hidden), lambda i: (0, 0))],
        out_shape=(
            shape16(2, own, 2 * hidden),
            shape16(2, own, 2 * hidden),
            shape32(own, width),
            shape16(own, width),
            shape32(8, 2 * hidden),
        ),
        compiler_params=ROOM,
        cost_estimate=cost(12 * 2 * own * width * hidden, own * hidden * 12 + width * hidden * 8, 4 * own * hidden),
        name="mlp",
    )(mine, other, top_a, top_b, up_a, up_b, down)


def turn_kernel(mine, other, hidden, cotangent, weights, gain, a, b, hidden_grad, grad_attn, near, far, sums, c, d):
    half = weights.shape[0] // 2
    second_grad = mine[...] + wide(other[...])
    normed, scale = normalized(hidden[...])
    top = wide(cotangent[...])
    total = top + norm_back(normed, scale, second_grad * gain[...])
    hidden_grad[...] = total
    grad = low(total)
    grad_attn[...] = grad
    near[...] = low(dot32(grad, weights[:half, :], NT))
    far[...] = low(dot32(grad, weights[half:, :], NT))
    sums[0:1, :] = jnp.sum(wide(grad), axis=0, keepdims=True)
    sums[1:2, :] = jnp.sum(second_grad * normed, axis=0, keepdims=True)
    sums[2:3, :] = jnp.sum(second_grad, axis=0, keepdims=True)
    sums[3:4, :] = jnp.sum(top, axis=0, keepdims=True)


def turn(mine, other, hidden, cotangent, weights, gain, through):
    own, width = mine.shape
    half = weights.shape[0] // 2
    operands = (mine, other, hidden, cotangent, weights, gain[None])
    outs = (mine, other, shape16(own, half), shape16(own, half), shape32(4, width))
    return pl.pallas_call(
        turn_kernel,
        grid=(1,),
        in_specs=[full_spec(array) for array in operands] + [ANYWHERE] * 2,
        out_specs=[full_spec(array) for array in outs] + [ANYWHERE] * 2,
        out_shape=(
            shape32(own, width),
            shape16(own, width),
            shape16(own, half),
            shape16(own, half),
            shape32(4, width),
            *(jax.ShapeDtypeStruct(t.shape, t.dtype) for t in through),
        ),
        input_output_aliases={6: 5, 7: 6},
        compiler_params=ROOM,
        cost_estimate=cost(2 * own * width * width, own * width * 20),
        name="turn",
    )(*operands, *through)


def head_part(me, mask, own, first, last, weights):
    start = pl.multiple_of(jnp.bitwise_xor(me[0], mask) * own, own)
    cut = first.shape[1]
    depth = weights.shape[0] - PAD
    return dot32(first[pl.ds(start, own), :], weights[:depth, :cut], NT) + dot32(
        last[pl.ds(start, own), :], weights[:depth, cut:], NT
    )


def far_kernel(me, first, last, weights, chip, diagonal):
    own = chip.shape[0]
    diagonal[...] = low(head_part(me, 3, own, first, last, weights))
    chip[...] = head_part(me, 2, own, first, last, weights)


def near_kernel(
    me, first, last, weights, chip, diagonal, t0, t1, t2, t3, mine, core, sums, bias_sum, normed_s, arrived
):
    own = chip.shape[0]
    copies = [pltpu.make_async_copy(t, normed_s.at[k], arrived.at[k]) for k, t in enumerate((t0, t1, t2, t3))]
    for copy in copies:
        copy.start()
    gain_sum, shift_sum = 0.0, 0.0
    for m, copy in enumerate(copies):
        if m < 2:
            part = head_part(me, m, own, first, last, weights)
            out = core if m else mine
            out[...] = part.astype(out.dtype)
        else:
            part = wide((diagonal if m == 3 else chip)[...])
        copy.wait()
        gain_sum = gain_sum + jnp.sum(part * wide(normed_s[m]), axis=0, keepdims=True)
        shift_sum = shift_sum + jnp.sum(part, axis=0, keepdims=True)
    sums[0:1, :] = gain_sum
    sums[1:2, :] = shift_sum
    heads = bias_sum.shape[1] // HD
    for source, base in ((first, 0), (last, heads - 1)):
        total = jnp.sum(wide(source[...]), axis=0, keepdims=True)
        for h in range(source.shape[1] // (3 * HD)):
            for row, kind in ((0, 0), (1, 2)):
                at = (3 * h + kind) * HD
                bias_sum[row : row + 1, (base + h) * HD : (base + h + 1) * HD] = total[:, at : at + HD]


def finish_kernel(first, last, out, vectors):
    rows = out.shape[1]
    heads = out.shape[2] // HD
    for source, base in ((first, 0), (last, heads - 1)):
        total = wide(source[0])
        for k in range(1, source.shape[0]):
            total = total + wide(source[k])
        if base:
            vectors[...] = total[rows:, :]
        for h in range(source.shape[2] // (3 * HD)):
            for kind in range(3):
                at = (3 * h + kind) * HD
                out[kind, :, (base + h) * HD : (base + h + 1) * HD] = total[:rows, at : at + HD]


def last_kernel(mine, core, chip, tokens, hidden_grad, gain, out):
    normed, scale = normalized(wide(tokens[...]))
    grad = (mine[...] + wide(core[...]) + wide(chip[...])) * gain[...]
    out[...] = hidden_grad[...] + norm_back(normed, scale, grad)


def call(kernel, out_shape, flops, size, *operands, scalar=None, direct=(), deps=(), scratch=(), name=None):
    specs = [full_spec(array) for array in operands] + [ANYWHERE] * (len(direct) + len(deps))
    operands = operands + tuple(direct)
    outs = tuple(full_spec(shape) for shape in out_shape) if isinstance(out_shape, tuple) else full_spec(out_shape)
    count = len(operands)
    if scalar is not None:
        specs = [SCALAR] + specs
        operands = (scalar.reshape(1),) + operands
        count += 1
    skip = len(deps)

    def body(*refs):
        kernel(*refs[:count], *refs[count + skip :])

    return pl.pallas_call(
        body,
        grid=(1,),
        out_shape=out_shape,
        in_specs=specs,
        out_specs=outs,
        scratch_shapes=scratch,
        compiler_params=ROOM,
        cost_estimate=cost(flops, size),
        name=name or kernel.__name__,
    )(*operands, *deps)


def turned_rows_kernel(left, right, out):
    out[...] = low(jnp.transpose(dot32(right[...], left[...], TN)))


def gate_kernel(*refs):
    pass


def gate(values, *deps):
    return pl.pallas_call(
        gate_kernel,
        in_specs=[ANYWHERE] * (1 + len(deps)),
        out_specs=ANYWHERE,
        out_shape=jax.ShapeDtypeStruct(values.shape, values.dtype),
        input_output_aliases={0: 0},
        name="gate",
    )(values, *deps)


def plain(values):
    return with_layout_constraint(values, Layout(major_to_minor=tuple(range(values.ndim))))


def flip(values, axis, mask):
    size = lax.axis_size(axis)
    return plain(lax.ppermute(plain(values), axis, [(i, i ^ mask) for i in range(size)]))


def core_swap(values):
    return flip(values, "tensor", 1)


def chip_swap(values):
    return flip(values, "tensor", 2)


def place(buffer, piece, index):
    return lax.dynamic_update_slice_in_dim(buffer, piece[None], index, 0)


def pick(blocks, index):
    return lax.dynamic_index_in_dim(blocks, index, 0, keepdims=False)


def swap_blocks(whole):
    blocks = low(whole).reshape((lax.axis_size("dp"), -1) + whole.shape[1:])
    return lax.all_to_all(plain(blocks), "dp", 0, 0, tiled=True)


def halves(whole):
    size = lax.axis_size("dp")
    me = lax.axis_index("dp")
    blocks = whole.reshape((size // 2, 2, -1) + whole.shape[1:])
    keep = lax.dynamic_index_in_dim(blocks, me % 2, 1, keepdims=False)
    return keep, low(lax.dynamic_index_in_dim(blocks, 1 - me % 2, 1, keepdims=False))


def sum_column(column, sent):
    size = lax.axis_size("dp")
    me = lax.axis_index("dp")
    total = pick(column, me // 2)
    for mask in range(2, size, 2):
        total = total + wide(flip(pick(sent, (me ^ mask) // 2), "dp", mask))
    return total


def contract_rows(left_mat, right_mat):
    return dot32(left_mat, right_mat, TN)


def on_device(
    tokens,
    segment,
    cotangent,
    ln1_gain,
    ln1_bias,
    w_qkv,
    qv_bias,
    w_out,
    out_bias,
    ln2_gain,
    ln2_bias,
    w_up,
    up_bias,
    w_down,
    down_bias,
):
    dp = lax.axis_size("dp")
    place_dp = lax.axis_index("dp")
    me = lax.axis_index("tensor")
    own, width = tokens.shape
    rows_shard = w_qkv.shape[1]
    span = w_qkv.shape[2]
    hidden = w_up.shape[1]

    heads = span // HD

    out_turned = w_out.T
    out_turned_chip = chip_swap(out_turned)
    qkv_pack = pack([w_qkv], spread(qv_bias, PAD), kernel=pack_heads_kernel)
    from_core = core_swap(tokens)
    from_chip = chip_swap(tokens)
    top_core = core_swap(cotangent)
    first_norm, normed_own = first_norm_of(tokens, ln1_gain, ln1_bias, me, qkv_pack)
    first_norm, normed_core = first_norm_of(from_core, ln1_gain, ln1_bias, me ^ 1, normed_own, first_norm)
    (qkv_column,) = columns(qkv_pack, ((0, 3 * span + HD),), (normed_core,))
    from_chip = gate(from_chip, qkv_column)
    from_diagonal = core_swap(from_chip)

    edges = (0, hidden, hidden + 2 * span, 2 * hidden + 2 * span + HD)
    cuts = tuple(zip(edges, edges[1:]))
    rest_pack = pack(
        [w_down.T, out_turned, out_turned_chip, w_up], spread(up_bias, PAD), deps=(qkv_column, top_core)
    )
    bias_at = tuple(3 * h + kind for kind in (0, 2) for h in range(heads))
    (qkv_full,) = lay(qkv_column, (3 * span,), bias_at, deps=(rest_pack,))
    first_norm, normed_chip = first_norm_of(from_chip, ln1_gain, ln1_bias, me ^ 2, qkv_full, first_norm)
    first_norm, normed_diagonal = first_norm_of(from_diagonal, ln1_gain, ln1_bias, me ^ 3, normed_chip, first_norm)
    first_norm = first_norm.reshape(4 * own, width)

    seg_row = segment[None, :]
    split = project(first_norm, qkv_full)
    heads_out, log_totals = [], []
    for head in range(heads):
        deps = () if head == 0 else (up_column, heads_out[-1])
        out, log_total = attend(split, head, seg_row, deps)
        heads_out.append(out)
        log_totals.append(log_total)
        if head == 0:
            down_column, out_column, up_column = columns(rest_pack, cuts, (out,))

    (up_own,) = lay(up_column, (hidden,), tuple(range(hidden // HD)), deps=(heads_out[-1],))
    down_columns = beside(down_column, chip_swap(down_column), deps=(up_own,))
    mixed_own, mixed_chip, to_core = call(
        deal_kernel,
        (shape16(own, span), shape16(own, span), shape16(2, own, span)),
        0,
        own * span * 24,
        *heads_out,
        scalar=me,
        deps=(down_columns,),
    )
    mixed_core = core_swap(to_core)
    mixed_far = beside(mixed_chip, mixed_core[1])
    (out_pair,) = lay(out_column, (2 * span,), turned=True, deps=(mixed_far,))
    mixed_far = chip_swap(mixed_far)
    out_core = core_swap(out_pair)
    hidden_one, second, out_full = join(
        mixed_own, mixed_core, mixed_far, out_pair, out_core, tokens, out_bias, ln2_gain, ln2_bias, (up_own,)
    )
    (down_pair,) = lay(down_columns, (2 * hidden,), deps=(second,))

    up_chip = gate(chip_swap(up_own), down_pair)
    second_core = gate(core_swap(second), up_chip)
    active, pre_grad, second_own, second_far, up_bias_sum = mlp(
        second, second_core, cotangent, top_core, up_own, up_chip, down_pair
    )

    few = lax.axis_size("dp") <= FEW
    hidden_grad, grad_attn, grad_near, grad_far, turn_sums, active, pre_grad = turn(
        second_own, core_swap(second_far), hidden_one, cotangent, out_full, ln2_gain, (active, pre_grad)
    )
    down_whole = contract_rows(cotangent, active[0]) + contract_rows(top_core, active[1])
    down_keep, down_give = halves(down_whole) if few else (None, low(down_whole))
    grad_far = chip_swap(grad_far)
    grad_core = core_swap(beside_stack(grad_near, grad_far))

    up_whole = contract_rows(second, pre_grad[0]) + contract_rows(second_core, pre_grad[1])
    up_chip_grad = chip_swap(gate(low(up_whole[:, hidden:]), grad_far))

    out_part_near = contract_rows(beside(mixed_own, mixed_core[0]), grad_attn)
    out_part_far = contract_rows(mixed_far, grad_attn)
    out_core_grad = core_swap(low(jnp.stack([out_part_near[span:], out_part_far[span:]])))
    out_mid = low(out_part_far[:span] + wide(out_core_grad[1]))
    out_grad = out_part_near[:span] + wide(out_core_grad[0]) + wide(chip_swap(out_mid))
    up_out_whole = jnp.concatenate([up_whole[:, :hidden] + wide(up_chip_grad), out_grad.T], axis=1)

    def back(head, earlier, deps):
        return attend_back(
            split,
            head,
            heads_out[head],
            grad_near,
            grad_core,
            grad_far,
            log_totals[head],
            seg_row,
            earlier,
            deps,
        )

    grads = [back(0, (), (out_mid,))]
    if few:
        down_column = wide(down_keep) + wide(gate(flip(down_give, "dp", 1), grads[0]))
        down_sent = low(down_column)
        up_keep, up_give = halves(up_out_whole)
    for head in range(1, heads):
        last = head == heads - 1
        deps = tuple(grads[-1:]) if last else (down_sent,) if few else ()
        if last:
            first_whole = low(contract_rows(first_norm, grads[-1]))
            deps += (first_whole, up_give) if few else (first_whole,)
        grads.append(back(head, () if last else tuple(grads), deps))
    first_heads, last_head = grads[-2:]
    first_blocks = swap_blocks(first_whole)
    if few:
        up_column = wide(up_keep) + wide(flip(up_give, "dp", 1))
        up_sent = low(up_column)
        down_part = sum_column(down_column, down_sent)
    else:
        down_part = jnp.sum(wide(swap_blocks(down_give)), axis=0)
        up_sent = swap_blocks(up_out_whole)

    far_size = own * width * 8
    part_chip, part_diagonal = call(
        far_kernel,
        (shape32(own, width), shape16(own, width)),
        own * width * span * 12,
        far_size,
        first_heads,
        last_head,
        qkv_full,
        scalar=me,
    )
    from_diagonal = gate(core_swap(part_diagonal), up_sent, down_part, first_blocks)
    chip_sum = low(part_chip + wide(from_diagonal))
    last_whole = call(turned_rows_kernel, shape16(width, 3 * HD), 0, own * width * 8, first_norm, last_head)
    part_own, part_core, first_sums, bias_sum = call(
        near_kernel,
        (shape32(own, width), shape16(own, width), shape32(2, width), shape32(2, span)),
        own * width * span * 12,
        far_size * 2,
        first_heads,
        last_head,
        qkv_full,
        part_chip,
        part_diagonal,
        scalar=me,
        direct=(normed_own, normed_core, normed_chip, normed_diagonal),
        scratch=[pltpu.VMEM((4, own, width), jnp.bfloat16), pltpu.SemaphoreType.DMA((4,))],
        deps=(chip_sum, last_whole),
    )
    chip_sum = chip_swap(chip_sum)

    bias_spread = place(jnp.zeros((4, 2, span), jnp.float32), bias_sum, me)
    up_rows = place(jnp.zeros((4, hidden), jnp.float32), up_bias_sum[0, :hidden], me)
    up_rows = place(up_rows, up_bias_sum[0, hidden:], me ^ 2)
    sums = jnp.concatenate(
        [first_sums, turn_sums, bias_spread.reshape(-1, width), up_rows.reshape(-1, width)], axis=0
    )
    up_out = sum_column(up_column, up_sent) if few else jnp.sum(wide(up_sent), axis=0)
    packed = gate(low(sums).reshape(-1, 3 * HD), up_out, chip_sum)
    last_blocks = lax.all_to_all(
        plain(
            jnp.concatenate(
                [last_whole.reshape(dp, rows_shard, 3 * HD), jnp.broadcast_to(packed, (dp,) + packed.shape)], axis=1
            )
        ),
        "dp",
        0,
        0,
        tiled=True,
    )
    down_grad_out = (down_part[:, :hidden] + wide(chip_swap(low(down_part[:, hidden:])))).T
    up_grad_out = up_out[:, :hidden]
    w_out_grad_out = up_out[:, hidden:].T

    active = gate(active.reshape(2 * own, 2 * hidden), packed)
    mlp_part = dot32(active, down_pair, NT)
    mlp_branch = mlp_part[:own] + wide(core_swap(low(mlp_part[own:])))
    block_out = hidden_one + (mlp_branch + wide(down_bias))

    (token_grad,) = call(
        last_kernel,
        (shape32(own, width),),
        own * width * 30,
        own * width * 16,
        part_own,
        core_swap(part_core),
        chip_sum,
        tokens,
        hidden_grad,
        ln1_gain[None],
    )

    w_qkv_grad_out, packed = call(
        finish_kernel,
        (shape32(3, rows_shard, span), shape32(*packed.shape)),
        0,
        width * span * 6,
        first_blocks,
        last_blocks,
        deps=(token_grad,),
    )
    sums = packed.reshape(sums.shape)
    sums = sums + core_swap(sums) + chip_swap(sums) + flip(sums, "tensor", 3)

    count = bias_spread.size // width
    qv_bias_grad = pick(sums[6 : 6 + count].reshape((4, 2, span // HD, dp, qv_bias.shape[2])), me)
    qv_bias_grad = lax.dynamic_index_in_dim(qv_bias_grad, place_dp, 2, keepdims=False)
    up_bias_grad = pick(sums[6 + count :].reshape((4, hidden // HD, dp, up_bias.shape[1])), me)
    up_bias_grad = lax.dynamic_index_in_dim(up_bias_grad, place_dp, 1, keepdims=False)
    return (
        block_out,
        token_grad,
        sums[0],
        sums[1],
        w_qkv_grad_out,
        qv_bias_grad,
        w_out_grad_out,
        sums[2],
        sums[3],
        sums[4],
        up_grad_out,
        up_bias_grad,
        down_grad_out,
        sums[5],
    )


def solution(mesh):
    in_specs = (
        P(("dp", "tensor"), None),
        P("dp"),
        P(("dp", "tensor"), None),
        P(),
        P(),
        P(None, "dp", "tensor"),
        P(None, "tensor", "dp"),
        P("tensor", "dp"),
        P(),
        P(),
        P(),
        P("dp", "tensor"),
        P("tensor", "dp"),
        P("tensor", "dp"),
        P(),
    )
    out_specs = (
        P(("dp", "tensor"), None),
        P(("dp", "tensor"), None),
        P(),
        P(),
        P(None, "dp", "tensor"),
        P(None, "tensor", "dp"),
        P("tensor", "dp"),
        P(),
        P(),
        P(),
        P("dp", "tensor"),
        P("tensor", "dp"),
        P("tensor", "dp"),
        P(),
    )
    return jax.shard_map(
        on_device, mesh=mesh, in_specs=in_specs, out_specs=out_specs, check_vma=False
    )
```

```python
import functools

import jax
import jax.numpy as jnp
from jax import lax
from jax.experimental import pallas as pl
from jax.experimental.layout import Layout, with_layout_constraint
from jax.experimental.pallas import tpu as pltpu
from jax.sharding import PartitionSpec as P

HD = 64
BLK = 256
EDGE = 512
FEW = 8
PAD = 16
EPSILON = 1e-05
GELU_COEF = 0.7978845608028654
NT = (((1,), (1,)), ((), ()))
TN = (((0,), (0,)), ((), ()))
NN = (((1,), (0,)), ((), ()))
ROOM = pltpu.CompilerParams(vmem_limit_bytes=48 * 2**20)
SCALAR = pl.BlockSpec(memory_space=pltpu.SMEM)
ANYWHERE = pl.BlockSpec(memory_space=pl.ANY)


def low(values):
    return values.astype(jnp.bfloat16)


def wide(values):
    return values.astype(jnp.float32)


def shape16(*dims):
    return jax.ShapeDtypeStruct(dims, jnp.bfloat16)


def shape32(*dims):
    return jax.ShapeDtypeStruct(dims, jnp.float32)


def cost(flops, size, exps=0):
    return pl.CostEstimate(flops=1, bytes_accessed=1, transcendentals=0)


def dot32(left, right, dims):
    return lax.dot_general(left, right, dims, preferred_element_type=jnp.float32)


def normalized(values_in):
    row_mean = jnp.mean(values_in, axis=-1, keepdims=True)
    centered = values_in - row_mean
    variance = jnp.mean(centered * centered, axis=-1, keepdims=True)
    scale = lax.rsqrt(variance + EPSILON)
    return centered * scale, scale


def norm_back(normed, scale, grad):
    mean_grad = jnp.mean(grad, axis=-1, keepdims=True)
    mean_both = jnp.mean(grad * normed, axis=-1, keepdims=True)
    return scale * (grad - mean_grad - normed * mean_both)


def first_kernel(index, piece, gain, shift, *rest):
    normed, _ = normalized(wide(piece[...]))
    rest[-2][0] = low(normed * gain[...] + shift[...])
    rest[-1][...] = low(normed)


def first_norm_of(piece, gain, shift, index, dep, buffer=None):
    own, width = piece.shape
    steps = 2
    rows = own // steps
    row_spec = pl.BlockSpec((1, width), lambda i, at: (0, 0))
    operands = [index.reshape(1), piece, gain[None], shift[None], dep]
    in_specs = [pl.BlockSpec((rows, width), lambda i, at: (i, 0)), row_spec, row_spec, ANYWHERE]
    aliases = {}
    if buffer is not None:
        operands.append(buffer)
        in_specs.append(ANYWHERE)
        aliases = {5: 0}
    return pl.pallas_call(
        first_kernel,
        grid_spec=pltpu.PrefetchScalarGridSpec(
            num_scalar_prefetch=1,
            grid=(steps,),
            in_specs=in_specs,
            out_specs=[
                pl.BlockSpec((1, rows, width), lambda i, at: (at[0], i, 0)),
                pl.BlockSpec((rows, width), lambda i, at: (i, 0)),
            ],
        ),
        out_shape=(shape16(4, own, width), shape16(own, width)),
        input_output_aliases=aliases,
        cost_estimate=cost(own * width * 12, own * width * 4),
        name="first_norm",
    )(*operands)


def pack_kernel(*refs):
    out = refs[-1]
    at = 0
    for ref in refs[:-2]:
        out[:, at : at + ref.shape[1]] = ref[...]
        at += ref.shape[1]
    out[:, at:] = jnp.zeros((out.shape[0], out.shape[1] - at), out.dtype)
    tail = refs[-2]
    count = min(tail.shape[0], out.shape[0])
    out[:count, at : at + tail.shape[1]] = tail[:count, :]


def pack_heads_kernel(weights, tail, out):
    kinds, height, span = weights.shape
    for h in range(span // HD):
        for k in range(kinds):
            at = (h * kinds + k) * HD
            out[:, at : at + HD] = weights[k, :, h * HD : (h + 1) * HD]
    out[:, kinds * span :] = jnp.zeros((height, tail.shape[1]), out.dtype)
    count = min(tail.shape[0], height)
    out[:count, kinds * span :] = tail[:count, :]


def pack(arrays, tail, deps=(), kernel=pack_kernel):
    width = sum(a.shape[-1] * (a.shape[0] if a.ndim == 3 else 1) for a in arrays) + tail.shape[1]
    height = arrays[0].shape[-2]
    return call(kernel, shape16(height, width), 0, height * width * 4, *arrays, tail, deps=deps)


def column_kernel(cuts, *refs):
    outs = refs[len(refs) - len(cuts) :]
    for k, ref in enumerate(refs[: len(refs) - len(cuts)]):
        for out, (first, last) in zip(outs, cuts):
            out[k] = ref[:, first:last]


def columns(shard, cuts, deps=()):
    size = lax.axis_size("dp")
    if size > FEW:
        pieces = lax.all_gather(shard, "dp")
        return [pieces[:, :, first:last] for first, last in cuts]
    near = [shard] + [flip(shard, "dp", mask) for mask in range(2, size, 2)]
    rows = shard.shape[0]
    return call(
        functools.partial(column_kernel, cuts),
        tuple(shape16(len(near), rows, last - first) for first, last in cuts),
        0,
        shard.size * 16,
        *near,
        deps=deps,
        name="columns",
    )


def beside_kernel(*refs):
    at = 0
    for ref in refs[:-1]:
        refs[-1][..., at : at + ref.shape[-1]] = ref[...]
        at += ref.shape[-1]


def beside(*arrays, deps=()):
    width = sum(a.shape[-1] for a in arrays)
    return call(beside_kernel, shape16(*arrays[0].shape[:-1], width), 0, arrays[0].size * 8, *arrays, deps=deps)


def core_stack_kernel(near, far, out):
    out[0] = near[:, out.shape[2] :]
    out[1] = far[:, out.shape[2] :]


def beside_stack(near, far):
    own, width = near.shape
    return call(core_stack_kernel, shape16(2, own, width // 2), 0, own * width * 4, near, far)


def lay_kernel(spans, bias_at, turned, me, near, other, *outs):
    count, rows = near.shape[:2]
    z, x = me[0] // 2, me[0] % 2
    total = None
    for m in range(count):
        slot = 2 * jnp.bitwise_xor(z, m)
        for at, source in ((slot + x, near), (slot + 1 - x, other)):
            start = pl.multiple_of(at * rows, 16)
            first = 0
            for k, span in enumerate(spans):
                out = outs[-1] if turned and k == len(spans) - 1 else outs[k]
                out[pl.ds(start, rows), :] = source[m, :, first : first + span].astype(out.dtype)
                first += span
            if bias_at:
                row = wide(source[m, 0:PAD, first : first + HD])
                total = row if total is None else total + row
    if turned:
        outs[len(spans) - 1][...] = low(jnp.transpose(outs[-1][...]))
    if bias_at:
        out = outs[0]
        below = slice(2 * count * rows, 2 * count * rows + PAD)
        out[below, :] = jnp.zeros((PAD, out.shape[1]), out.dtype)
        for k, at in enumerate(bias_at):
            out[below, at * HD : (at + 1) * HD] = low(jnp.broadcast_to(total[k : k + 1, :], (PAD, HD)))


def lay(near, spans, bias_at=(), turned=False, deps=()):
    size = lax.axis_size("dp")
    rows = near.shape[1]
    if size > FEW:
        whole = near.reshape(size * rows, -1)
        outs, first = [], 0
        for span in spans:
            outs.append(whole[:, first : first + span])
            first += span
        if turned:
            outs[-1] = outs[-1].T
        if bias_at:
            total = jnp.sum(wide(near[:, :, first : first + HD]), axis=0)[: len(bias_at)]
            total = jnp.zeros((spans[0] // HD, HD), jnp.float32).at[jnp.array(bias_at)].set(total)
            outs[0] = jnp.concatenate([outs[0], low(jnp.broadcast_to(total.reshape(1, -1), (PAD, spans[0])))], axis=0)
        return outs
    other = flip(near, "dp", 1)
    shapes = [shape16(size * rows, span) for span in spans]
    if turned:
        shapes[-1] = shape16(spans[-1], size * rows)
    if bias_at:
        shapes[0] = shape16(size * rows + PAD, spans[0])
    return call(
        functools.partial(lay_kernel, spans, bias_at, turned),
        tuple(shapes),
        0,
        near.size * 8,
        near,
        other,
        scalar=lax.axis_index("dp"),
        deps=deps,
        scratch=[pltpu.VMEM((size * rows, spans[-1]), jnp.float32)] if turned else [],
        name="lay",
    )


def spread(bias, rows):
    dp = lax.axis_size("dp")
    mine = lax.broadcasted_iota(jnp.int32, (1, dp, 1), 1) == lax.axis_index("dp")
    shard = bias.reshape(-1, 1, bias.shape[-1])
    placed = jnp.where(mine, shard, jnp.zeros((), bias.dtype)).reshape(shard.shape[0], HD)
    return jnp.concatenate([placed, jnp.zeros((rows - placed.shape[0], HD), bias.dtype)], axis=0)


def one_document(row_total, block_a, block_b):
    first, last = EDGE // BLK, (row_total - EDGE) // BLK
    return first <= block_a < last and first <= block_b < last


def project_kernel(normed, weights, out):
    heads = out.shape[0] // 3
    width = heads * HD
    depth = normed.shape[1]
    part = low(dot32(normed[...], weights[:depth, :], NN) + wide(weights[depth : depth + PAD, :])[0:1, :])
    for h in range(heads):
        for k in range(3):
            one = part[:, (h * 3 + k) * HD : (h * 3 + k + 1) * HD]
            out[k * heads + h] = one if k else low(wide(one) * HD ** -0.5)


def project(normed, weights):
    rows, depth = normed.shape
    count = weights.shape[1] // HD
    return pl.pallas_call(
        project_kernel,
        grid=(4,),
        in_specs=[
            pl.BlockSpec((rows // 4, depth), lambda i: (i, 0)),
            pl.BlockSpec(weights.shape, lambda i: (0, 0)),
        ],
        out_specs=pl.BlockSpec((count, rows // 4, HD), lambda i: (0, i, 0)),
        out_shape=shape16(count, rows, HD),
        compiler_params=ROOM,
        cost_estimate=cost(2 * rows * depth * count * HD, rows * depth * 6),
        name="project",
    )(normed, weights)


def attend_kernel(count, query_ref, key_ref, value_ref, seg_row, *refs):
    out, lse, c_s = refs[count], refs[count + 1], refs[count + 2]
    rows = out.shape[0]
    c_s[...] = jnp.transpose(jnp.broadcast_to(seg_row[...], (128, rows)))
    for i in range(rows // BLK):
        mine = pl.ds(i * BLK, BLK)
        query = query_ref[0, mine, :]
        seg_mine = c_s[mine, :]
        seg_mine = jnp.concatenate([seg_mine, seg_mine], axis=1)
        tiles = []
        for j in range(i + 1):
            other = pl.ds(j * BLK, BLK)
            score = dot32(query, key_ref[0, other, :], NT)
            allowed = None
            if not one_document(rows, i, j):
                allowed = seg_mine == seg_row[:, other]
            if i == j:
                causal = lax.broadcasted_iota(jnp.int32, (BLK, BLK), 1) <= lax.broadcasted_iota(
                    jnp.int32, (BLK, BLK), 0
                )
                allowed = causal if allowed is None else allowed & causal
            if allowed is not None:
                score = jnp.where(allowed, score, -1e30)
            tiles.append(score)
        top = tiles[0]
        for tile in tiles[1:]:
            top = jnp.maximum(top, tile)
        top = jnp.max(top, axis=1, keepdims=True)
        total = None
        mixed = None
        for j, tile in enumerate(tiles):
            weight = jnp.exp(tile - top)
            total = weight if total is None else total + weight
            term = dot32(low(weight), value_ref[0, pl.ds(j * BLK, BLK), :], NN)
            mixed = term if mixed is None else mixed + term
        total = jnp.sum(total, axis=1, keepdims=True)
        out[mine, :] = low(mixed / total)
        log_total = jnp.broadcast_to(top + jnp.log(total), (BLK, 128))
        lse[:, mine] = jnp.transpose(log_total)[0:8, :]


def head_specs(split, head, count):
    rows = split.shape[1]
    return [
        pl.BlockSpec((1, rows, HD), lambda i, k=k: (k * count + head, 0, 0)) for k in range(3)
    ]


def full_spec(array):
    return pl.BlockSpec(array.shape, lambda i: (0,) * array.ndim)


def attend(split, head, seg_row, deps=()):
    count, rows = split.shape[0] // 3, split.shape[1]
    return pl.pallas_call(
        functools.partial(attend_kernel, len(deps)),
        grid=(1,),
        in_specs=head_specs(split, head, count) + [full_spec(seg_row)] + [ANYWHERE] * len(deps),
        out_specs=[pl.BlockSpec((rows, HD), lambda i: (0, 0)), pl.BlockSpec((8, rows), lambda i: (0, 0))],
        out_shape=(shape16(rows, HD), shape32(8, rows)),
        scratch_shapes=[pltpu.VMEM((rows, 128), jnp.int32)],
        compiler_params=ROOM,
        cost_estimate=cost(7e9, rows * 1024, rows * rows // 2),
        name="attend",
    )(split, split, split, seg_row, *deps)


def deal_kernel(me, *refs):
    heads, keep, chip, core = refs[:-3], refs[-3], refs[-2], refs[-1]
    own = keep.shape[0]
    for m, out in ((0, keep), (2, chip), (1, core.at[0]), (3, core.at[1])):
        start = pl.multiple_of(jnp.bitwise_xor(me[0], m) * own, own)
        for h, head in enumerate(heads):
            out[:, h * HD : (h + 1) * HD] = head[pl.ds(start, own), :]


def attend_back_kernel(
    head, count, extra, me, query_ref, key_ref, value_ref, mixed, near, core, far, lse, seg_row, *refs
):
    earlier, out = refs[:extra], refs[extra + count]
    g_s, d_s, dk_s, dv_s, c_s = refs[extra + count + 1 :]
    rows = mixed.shape[0]
    own = rows // 4
    lanes = slice(head * HD, (head + 1) * HD)
    for m, piece in enumerate((near[:, lanes], core[0, :, lanes], far[:, lanes], core[1, :, lanes])):
        start = pl.multiple_of(jnp.bitwise_xor(me[0], m) * own, own)
        g_s[pl.ds(start, own), :] = piece
    c_s[...] = jnp.transpose(jnp.broadcast_to(seg_row[...], (128, rows)))
    inner = jnp.sum(wide(mixed[...]) * wide(g_s[...]), axis=1, keepdims=True)
    d_s[...] = jnp.transpose(jnp.broadcast_to(inner, (rows, 128)))[0:8, :]
    def store(kind, where, values):
        at = (3 * extra + kind) * HD
        out[where, at : at + HD] = values

    for i in range(rows // BLK):
        mine = pl.ds(i * BLK, BLK)
        query = query_ref[0, mine, :]
        grad_mine = g_s[mine, :]
        log_total = lse[0:1, mine]
        inner = d_s[0:1, mine]
        query_grad = None
        for j in range(i + 1):
            other = pl.ds(j * BLK, BLK)
            key = key_ref[0, other, :]
            score = dot32(key, query, NT)
            weight = jnp.exp(score - log_total)
            allowed = None
            if not one_document(rows, i, j):
                seg_other = c_s[other, :]
                seg_other = jnp.concatenate([seg_other, seg_other], axis=1)
                allowed = seg_other == seg_row[:, mine]
            if i == j:
                causal = lax.broadcasted_iota(jnp.int32, (BLK, BLK), 0) <= lax.broadcasted_iota(
                    jnp.int32, (BLK, BLK), 1
                )
                allowed = causal if allowed is None else allowed & causal
            if allowed is not None:
                weight = jnp.where(allowed, weight, 0.0)
            weight_grad = dot32(value_ref[0, other, :], grad_mine, NT)
            score_grad = low(weight * (weight_grad - inner))
            value_term = dot32(low(weight), grad_mine, NN)
            key_term = dot32(score_grad, query, NN)
            query_term = dot32(score_grad, key, TN)
            query_grad = query_term if query_grad is None else query_grad + query_term
            if i == j:
                dv_s[other, :] = value_term
                dk_s[other, :] = key_term
            else:
                dv_s[other, :] += value_term
                dk_s[other, :] += key_term
        store(0, mine, low(query_grad * HD ** -0.5))
    store(1, slice(None), low(dk_s[...]))
    store(2, slice(None), low(dv_s[...]))
    for h, ref in enumerate(earlier):
        out[:, 3 * h * HD : 3 * (h + 1) * HD] = ref[...]


def attend_back(split, head, mixed, near, core, far, lse, seg_row, earlier=(), deps=()):
    count, rows = split.shape[0] // 3, split.shape[1]
    full = pltpu.VMEM((rows, HD), jnp.float32)
    operands = [mixed, near, core, far, lse, seg_row, *earlier]
    shape = shape16(rows, 3 * (len(earlier) + 1) * HD)
    return pl.pallas_call(
        functools.partial(attend_back_kernel, head, len(deps), len(earlier)),
        grid=(1,),
        in_specs=[SCALAR]
        + head_specs(split, head, count)
        + [full_spec(array) for array in operands]
        + [ANYWHERE] * len(deps),
        out_specs=full_spec(shape),
        out_shape=shape,
        scratch_shapes=[
            pltpu.VMEM((rows, HD), jnp.bfloat16),
            pltpu.VMEM((8, rows), jnp.float32),
            full,
            full,
            pltpu.VMEM((rows, 128), jnp.int32),
        ],
        compiler_params=ROOM,
        cost_estimate=cost(15e9, rows * 2048, rows * rows // 2),
        name="attend_back",
    )(lax.axis_index("tensor").reshape(1), split, split, split, *operands, *deps)


def join_kernel(near, core, far, mine, other, tokens, bias, gain, shift, hidden, second, weights):
    span = near.shape[1]
    for k, piece in enumerate((mine[:span, :], other[:span, :], mine[span:, :], other[span:, :])):
        weights[k * span : (k + 1) * span, :] = piece
    branch = (
        dot32(near[...], weights[:span, :], NN)
        + dot32(core[0], weights[span : 2 * span, :], NN)
        + dot32(far[...], weights[2 * span :, :], NN)
    )
    total = wide(tokens[...]) + (branch + wide(bias[...]))
    hidden[...] = total
    normed, _ = normalized(total)
    second[...] = low(normed * gain[...] + shift[...])


def join(near, core, far, mine, other, tokens, bias, gain, shift, deps):
    own, width = tokens.shape
    return call(
        join_kernel,
        (shape32(own, width), shape16(own, width), shape16(2 * mine.shape[0], width)),
        2 * own * width * width,
        own * width * 12,
        near,
        core,
        far,
        mine,
        other,
        tokens,
        bias[None],
        gain[None],
        shift[None],
        deps=deps,
    )


def mlp_kernel(mine, other, top_a, top_b, up_a, up_b, down, active, pre_grads, own_part, core_part, bias_sum):
    depth, hidden = down.shape[0], up_a.shape[1]

    @pl.when(pl.program_id(0) == 0)
    def _():
        bias_sum[...] = jnp.zeros_like(bias_sum)

    for k, (source, top) in enumerate(((mine, top_a), (other, top_b))):
        rows = source[...]
        grad = top[...]
        part = None
        for half, up in enumerate((up_a, up_b)):
            lanes = slice(half * hidden, (half + 1) * hidden)
            pre = dot32(rows, up[:depth, :], NN) + wide(up[depth : depth + PAD, :])[0:1, :]
            act_grad = dot32(grad, down[:, lanes], NN)
            square = pre * pre
            bend = jnp.tanh(pre * (GELU_COEF + (GELU_COEF * 0.044715) * square))
            above = 0.5 + 0.5 * bend
            active[k, :, lanes] = low(pre * above)
            slope = above + (pre * (0.5 - 0.5 * bend * bend)) * (
                GELU_COEF + (3.0 * GELU_COEF * 0.044715) * square
            )
            pre_grad = low(act_grad * slope)
            pre_grads[k, :, lanes] = pre_grad
            bias_sum[0:1, lanes] += jnp.sum(wide(pre_grad), axis=0, keepdims=True)
            term = dot32(pre_grad, up[:depth, :], NT)
            part = term if part is None else part + term
        if k == 0:
            own_part[...] = part
        else:
            core_part[...] = low(part)


def mlp(mine, other, top_a, top_b, up_a, up_b, down):
    own, width = mine.shape
    hidden = up_a.shape[1]
    steps = 2
    rows = own // steps

    def whole(array):
        return pl.BlockSpec(array.shape, lambda i: (0,) * array.ndim)

    row_spec = pl.BlockSpec((rows, width), lambda i: (i, 0))
    wide_spec = pl.BlockSpec((2, rows, 2 * hidden), lambda i: (0, i, 0))
    return pl.pallas_call(
        mlp_kernel,
        grid=(steps,),
        in_specs=[row_spec] * 4 + [whole(array) for array in (up_a, up_b, down)],
        out_specs=[wide_spec, wide_spec, row_spec, row_spec, pl.BlockSpec((8, 2 * hidden), lambda i: (0, 0))],
        out_shape=(
            shape16(2, own, 2 * hidden),
            shape16(2, own, 2 * hidden),
            shape32(own, width),
            shape16(own, width),
            shape32(8, 2 * hidden),
        ),
        compiler_params=ROOM,
        cost_estimate=cost(12 * 2 * own * width * hidden, own * hidden * 12 + width * hidden * 8, 4 * own * hidden),
        name="mlp",
    )(mine, other, top_a, top_b, up_a, up_b, down)


def turn_kernel(mine, other, hidden, cotangent, weights, gain, a, b, hidden_grad, grad_attn, near, far, sums, c, d):
    half = weights.shape[0] // 2
    second_grad = mine[...] + wide(other[...])
    normed, scale = normalized(hidden[...])
    top = wide(cotangent[...])
    total = top + norm_back(normed, scale, second_grad * gain[...])
    hidden_grad[...] = total
    grad = low(total)
    grad_attn[...] = grad
    near[...] = low(dot32(grad, weights[:half, :], NT))
    far[...] = low(dot32(grad, weights[half:, :], NT))
    sums[0:1, :] = jnp.sum(wide(grad), axis=0, keepdims=True)
    sums[1:2, :] = jnp.sum(second_grad * normed, axis=0, keepdims=True)
    sums[2:3, :] = jnp.sum(second_grad, axis=0, keepdims=True)
    sums[3:4, :] = jnp.sum(top, axis=0, keepdims=True)


def turn(mine, other, hidden, cotangent, weights, gain, through):
    own, width = mine.shape
    half = weights.shape[0] // 2
    operands = (mine, other, hidden, cotangent, weights, gain[None])
    outs = (mine, other, shape16(own, half), shape16(own, half), shape32(4, width))
    return pl.pallas_call(
        turn_kernel,
        grid=(1,),
        in_specs=[full_spec(array) for array in operands] + [ANYWHERE] * 2,
        out_specs=[full_spec(array) for array in outs] + [ANYWHERE] * 2,
        out_shape=(
            shape32(own, width),
            shape16(own, width),
            shape16(own, half),
            shape16(own, half),
            shape32(4, width),
            *(jax.ShapeDtypeStruct(t.shape, t.dtype) for t in through),
        ),
        input_output_aliases={6: 5, 7: 6},
        compiler_params=ROOM,
        cost_estimate=cost(2 * own * width * width, own * width * 20),
        name="turn",
    )(*operands, *through)


def head_part(me, mask, own, first, last, weights):
    start = pl.multiple_of(jnp.bitwise_xor(me[0], mask) * own, own)
    cut = first.shape[1]
    depth = weights.shape[0] - PAD
    return dot32(first[pl.ds(start, own), :], weights[:depth, :cut], NT) + dot32(
        last[pl.ds(start, own), :], weights[:depth, cut:], NT
    )


def far_kernel(me, first, last, weights, chip, diagonal):
    own = chip.shape[0]
    diagonal[...] = low(head_part(me, 3, own, first, last, weights))
    chip[...] = head_part(me, 2, own, first, last, weights)


def near_kernel(
    me, first, last, weights, chip, diagonal, t0, t1, t2, t3, mine, core, sums, bias_sum, normed_s, arrived
):
    own = chip.shape[0]
    copies = [pltpu.make_async_copy(t, normed_s.at[k], arrived.at[k]) for k, t in enumerate((t0, t1, t2, t3))]
    for copy in copies:
        copy.start()
    gain_sum, shift_sum = 0.0, 0.0
    for m, copy in enumerate(copies):
        if m < 2:
            part = head_part(me, m, own, first, last, weights)
            out = core if m else mine
            out[...] = part.astype(out.dtype)
        else:
            part = wide((diagonal if m == 3 else chip)[...])
        copy.wait()
        gain_sum = gain_sum + jnp.sum(part * wide(normed_s[m]), axis=0, keepdims=True)
        shift_sum = shift_sum + jnp.sum(part, axis=0, keepdims=True)
    sums[0:1, :] = gain_sum
    sums[1:2, :] = shift_sum
    heads = bias_sum.shape[1] // HD
    for source, base in ((first, 0), (last, heads - 1)):
        total = jnp.sum(wide(source[...]), axis=0, keepdims=True)
        for h in range(source.shape[1] // (3 * HD)):
            for row, kind in ((0, 0), (1, 2)):
                at = (3 * h + kind) * HD
                bias_sum[row : row + 1, (base + h) * HD : (base + h + 1) * HD] = total[:, at : at + HD]


def finish_kernel(first, last, out, vectors):
    rows = out.shape[1]
    heads = out.shape[2] // HD
    for source, base in ((first, 0), (last, heads - 1)):
        total = wide(source[0])
        for k in range(1, source.shape[0]):
            total = total + wide(source[k])
        if base:
            vectors[...] = total[rows:, :]
        for h in range(source.shape[2] // (3 * HD)):
            for kind in range(3):
                at = (3 * h + kind) * HD
                out[kind, :, (base + h) * HD : (base + h + 1) * HD] = total[:rows, at : at + HD]


def last_kernel(mine, core, chip, tokens, hidden_grad, gain, out):
    normed, scale = normalized(wide(tokens[...]))
    grad = (mine[...] + wide(core[...]) + wide(chip[...])) * gain[...]
    out[...] = hidden_grad[...] + norm_back(normed, scale, grad)


def call(kernel, out_shape, flops, size, *operands, scalar=None, direct=(), deps=(), scratch=(), name=None):
    specs = [full_spec(array) for array in operands] + [ANYWHERE] * (len(direct) + len(deps))
    operands = operands + tuple(direct)
    outs = tuple(full_spec(shape) for shape in out_shape) if isinstance(out_shape, tuple) else full_spec(out_shape)
    count = len(operands)
    if scalar is not None:
        specs = [SCALAR] + specs
        operands = (scalar.reshape(1),) + operands
        count += 1
    skip = len(deps)

    def body(*refs):
        kernel(*refs[:count], *refs[count + skip :])

    return pl.pallas_call(
        body,
        grid=(1,),
        out_shape=out_shape,
        in_specs=specs,
        out_specs=outs,
        scratch_shapes=scratch,
        compiler_params=ROOM,
        cost_estimate=cost(flops, size),
        name=name or kernel.__name__,
    )(*operands, *deps)


def turned_rows_kernel(left, right, out):
    out[...] = low(jnp.transpose(dot32(right[...], left[...], TN)))


def gate_kernel(*refs):
    pass


def gate(values, *deps):
    return pl.pallas_call(
        gate_kernel,
        in_specs=[ANYWHERE] * (1 + len(deps)),
        out_specs=ANYWHERE,
        out_shape=jax.ShapeDtypeStruct(values.shape, values.dtype),
        input_output_aliases={0: 0},
        name="gate",
    )(values, *deps)


def plain(values):
    return with_layout_constraint(values, Layout(major_to_minor=tuple(range(values.ndim))))


def flip(values, axis, mask):
    size = lax.axis_size(axis)
    return plain(lax.ppermute(plain(values), axis, [(i, i ^ mask) for i in range(size)]))


def core_swap(values):
    return flip(values, "tensor", 1)


def chip_swap(values):
    return flip(values, "tensor", 2)


def place(buffer, piece, index):
    return lax.dynamic_update_slice_in_dim(buffer, piece[None], index, 0)


def pick(blocks, index):
    return lax.dynamic_index_in_dim(blocks, index, 0, keepdims=False)


def swap_blocks(whole):
    blocks = low(whole).reshape((lax.axis_size("dp"), -1) + whole.shape[1:])
    return lax.all_to_all(plain(blocks), "dp", 0, 0, tiled=True)


def halves(whole):
    size = lax.axis_size("dp")
    me = lax.axis_index("dp")
    blocks = whole.reshape((size // 2, 2, -1) + whole.shape[1:])
    keep = lax.dynamic_index_in_dim(blocks, me % 2, 1, keepdims=False)
    return keep, low(lax.dynamic_index_in_dim(blocks, 1 - me % 2, 1, keepdims=False))


def sum_column(column, sent):
    size = lax.axis_size("dp")
    me = lax.axis_index("dp")
    total = pick(column, me // 2)
    for mask in range(2, size, 2):
        total = total + wide(flip(pick(sent, (me ^ mask) // 2), "dp", mask))
    return total


def contract_rows(left_mat, right_mat):
    return dot32(left_mat, right_mat, TN)


def on_device(
    tokens,
    segment,
    cotangent,
    ln1_gain,
    ln1_bias,
    w_qkv,
    qv_bias,
    w_out,
    out_bias,
    ln2_gain,
    ln2_bias,
    w_up,
    up_bias,
    w_down,
    down_bias,
):
    dp = lax.axis_size("dp")
    place_dp = lax.axis_index("dp")
    me = lax.axis_index("tensor")
    own, width = tokens.shape
    rows_shard = w_qkv.shape[1]
    span = w_qkv.shape[2]
    hidden = w_up.shape[1]

    heads = span // HD

    out_turned = w_out.T
    out_turned_chip = chip_swap(out_turned)
    qkv_pack = pack([w_qkv], spread(qv_bias, PAD), kernel=pack_heads_kernel)
    from_core = core_swap(tokens)
    from_chip = chip_swap(tokens)
    top_core = core_swap(cotangent)
    first_norm, normed_own = first_norm_of(tokens, ln1_gain, ln1_bias, me, qkv_pack)
    first_norm, normed_core = first_norm_of(from_core, ln1_gain, ln1_bias, me ^ 1, normed_own, first_norm)
    (qkv_column,) = columns(qkv_pack, ((0, 3 * span + HD),), (normed_core,))
    from_chip = gate(from_chip, qkv_column)
    from_diagonal = core_swap(from_chip)

    edges = (0, hidden, hidden + 2 * span, 2 * hidden + 2 * span + HD)
    cuts = tuple(zip(edges, edges[1:]))
    rest_pack = pack(
        [w_down.T, out_turned, out_turned_chip, w_up], spread(up_bias, PAD), deps=(qkv_column, top_core)
    )
    bias_at = tuple(3 * h + kind for kind in (0, 2) for h in range(heads))
    (qkv_full,) = lay(qkv_column, (3 * span,), bias_at, deps=(rest_pack,))
    first_norm, normed_chip = first_norm_of(from_chip, ln1_gain, ln1_bias, me ^ 2, qkv_full, first_norm)
    first_norm, normed_diagonal = first_norm_of(from_diagonal, ln1_gain, ln1_bias, me ^ 3, normed_chip, first_norm)
    first_norm = first_norm.reshape(4 * own, width)

    seg_row = segment[None, :]
    split = project(first_norm, qkv_full)
    heads_out, log_totals = [], []
    for head in range(heads):
        deps = () if head == 0 else (up_column, heads_out[-1])
        out, log_total = attend(split, head, seg_row, deps)
        heads_out.append(out)
        log_totals.append(log_total)
        if head == 0:
            down_column, out_column, up_column = columns(rest_pack, cuts, (out,))

    (up_own,) = lay(up_column, (hidden,), tuple(range(hidden // HD)), deps=(heads_out[-1],))
    down_columns = beside(down_column, chip_swap(down_column), deps=(up_own,))
    mixed_own, mixed_chip, to_core = call(
        deal_kernel,
        (shape16(own, span), shape16(own, span), shape16(2, own, span)),
        0,
        own * span * 24,
        *heads_out,
        scalar=me,
        deps=(down_columns,),
    )
    mixed_core = core_swap(to_core)
    mixed_far = beside(mixed_chip, mixed_core[1])
    (out_pair,) = lay(out_column, (2 * span,), turned=True, deps=(mixed_far,))
    mixed_far = chip_swap(mixed_far)
    out_core = core_swap(out_pair)
    hidden_one, second, out_full = join(
        mixed_own, mixed_core, mixed_far, out_pair, out_core, tokens, out_bias, ln2_gain, ln2_bias, (up_own,)
    )
    (down_pair,) = lay(down_columns, (2 * hidden,), deps=(second,))

    up_chip = gate(chip_swap(up_own), down_pair)
    second_core = gate(core_swap(second), up_chip)
    active, pre_grad, second_own, second_far, up_bias_sum = mlp(
        second, second_core, cotangent, top_core, up_own, up_chip, down_pair
    )

    few = lax.axis_size("dp") <= FEW
    hidden_grad, grad_attn, grad_near, grad_far, turn_sums, active, pre_grad = turn(
        second_own, core_swap(second_far), hidden_one, cotangent, out_full, ln2_gain, (active, pre_grad)
    )
    down_whole = contract_rows(cotangent, active[0]) + contract_rows(top_core, active[1])
    down_keep, down_give = halves(down_whole) if few else (None, low(down_whole))
    grad_far = chip_swap(grad_far)
    grad_core = core_swap(beside_stack(grad_near, grad_far))

    up_whole = contract_rows(second, pre_grad[0]) + contract_rows(second_core, pre_grad[1])
    up_chip_grad = chip_swap(gate(low(up_whole[:, hidden:]), grad_far))

    out_part_near = contract_rows(beside(mixed_own, mixed_core[0]), grad_attn)
    out_part_far = contract_rows(mixed_far, grad_attn)
    out_core_grad = core_swap(low(jnp.stack([out_part_near[span:], out_part_far[span:]])))
    out_mid = low(out_part_far[:span] + wide(out_core_grad[1]))
    out_grad = out_part_near[:span] + wide(out_core_grad[0]) + wide(chip_swap(out_mid))
    up_out_whole = jnp.concatenate([up_whole[:, :hidden] + wide(up_chip_grad), out_grad.T], axis=1)

    def back(head, earlier, deps):
        return attend_back(
            split,
            head,
            heads_out[head],
            grad_near,
            grad_core,
            grad_far,
            log_totals[head],
            seg_row,
            earlier,
            deps,
        )

    grads = [back(0, (), (out_mid,))]
    if few:
        down_column = wide(down_keep) + wide(gate(flip(down_give, "dp", 1), grads[0]))
        down_sent = low(down_column)
        up_keep, up_give = halves(up_out_whole)
    for head in range(1, heads):
        last = head == heads - 1
        deps = tuple(grads[-1:]) if last else (down_sent,) if few else ()
        if last:
            first_whole = low(contract_rows(first_norm, grads[-1]))
            deps += (first_whole, up_give) if few else (first_whole,)
        grads.append(back(head, () if last else tuple(grads), deps))
    first_heads, last_head = grads[-2:]
    first_blocks = swap_blocks(first_whole)
    if few:
        up_column = wide(up_keep) + wide(flip(up_give, "dp", 1))
        up_sent = low(up_column)
        down_part = sum_column(down_column, down_sent)
    else:
        down_part = jnp.sum(wide(swap_blocks(down_give)), axis=0)
        up_sent = swap_blocks(up_out_whole)

    far_size = own * width * 8
    part_chip, part_diagonal = call(
        far_kernel,
        (shape32(own, width), shape16(own, width)),
        own * width * span * 12,
        far_size,
        first_heads,
        last_head,
        qkv_full,
        scalar=me,
    )
    from_diagonal = gate(core_swap(part_diagonal), up_sent, down_part, first_blocks)
    chip_sum = low(part_chip + wide(from_diagonal))
    last_whole = call(turned_rows_kernel, shape16(width, 3 * HD), 0, own * width * 8, first_norm, last_head)
    part_own, part_core, first_sums, bias_sum = call(
        near_kernel,
        (shape32(own, width), shape16(own, width), shape32(2, width), shape32(2, span)),
        own * width * span * 12,
        far_size * 2,
        first_heads,
        last_head,
        qkv_full,
        part_chip,
        part_diagonal,
        scalar=me,
        direct=(normed_own, normed_core, normed_chip, normed_diagonal),
        scratch=[pltpu.VMEM((4, own, width), jnp.bfloat16), pltpu.SemaphoreType.DMA((4,))],
        deps=(chip_sum, last_whole),
    )
    chip_sum = chip_swap(chip_sum)

    bias_spread = place(jnp.zeros((4, 2, span), jnp.float32), bias_sum, me)
    up_rows = place(jnp.zeros((4, hidden), jnp.float32), up_bias_sum[0, :hidden], me)
    up_rows = place(up_rows, up_bias_sum[0, hidden:], me ^ 2)
    sums = jnp.concatenate(
        [first_sums, turn_sums, bias_spread.reshape(-1, width), up_rows.reshape(-1, width)], axis=0
    )
    up_out = sum_column(up_column, up_sent) if few else jnp.sum(wide(up_sent), axis=0)
    packed = gate(low(sums).reshape(-1, 3 * HD), up_out, chip_sum)
    last_blocks = plain(
        jnp.concatenate(
            [last_whole.reshape(dp, rows_shard, 3 * HD), jnp.broadcast_to(packed, (dp,) + packed.shape)], axis=1
        )
    )
    active = gate(active.reshape(2 * own, 2 * hidden), last_blocks)
    last_blocks = lax.all_to_all(last_blocks, "dp", 0, 0, tiled=True)
    down_grad_out = (down_part[:, :hidden] + wide(chip_swap(low(down_part[:, hidden:])))).T
    up_grad_out = up_out[:, :hidden]
    w_out_grad_out = up_out[:, hidden:].T

    mlp_part = dot32(active, down_pair, NT)
    mlp_branch = mlp_part[:own] + wide(core_swap(low(mlp_part[own:])))
    block_out = hidden_one + (mlp_branch + wide(down_bias))

    (token_grad,) = call(
        last_kernel,
        (shape32(own, width),),
        own * width * 30,
        own * width * 16,
        part_own,
        core_swap(part_core),
        chip_sum,
        tokens,
        hidden_grad,
        ln1_gain[None],
    )

    w_qkv_grad_out, packed = call(
        finish_kernel,
        (shape32(3, rows_shard, span), shape32(*packed.shape)),
        0,
        width * span * 6,
        first_blocks,
        last_blocks,
        deps=(token_grad,),
    )
    sums = packed.reshape(sums.shape)
    sums = sums + core_swap(sums) + chip_swap(sums) + flip(sums, "tensor", 3)

    count = bias_spread.size // width
    qv_bias_grad = pick(sums[6 : 6 + count].reshape((4, 2, span // HD, dp, qv_bias.shape[2])), me)
    qv_bias_grad = lax.dynamic_index_in_dim(qv_bias_grad, place_dp, 2, keepdims=False)
    up_bias_grad = pick(sums[6 + count :].reshape((4, hidden // HD, dp, up_bias.shape[1])), me)
    up_bias_grad = lax.dynamic_index_in_dim(up_bias_grad, place_dp, 1, keepdims=False)
    return (
        block_out,
        token_grad,
        sums[0],
        sums[1],
        w_qkv_grad_out,
        qv_bias_grad,
        w_out_grad_out,
        sums[2],
        sums[3],
        sums[4],
        up_grad_out,
        up_bias_grad,
        down_grad_out,
        sums[5],
    )


def solution(mesh):
    in_specs = (
        P(("dp", "tensor"), None),
        P("dp"),
        P(("dp", "tensor"), None),
        P(),
        P(),
        P(None, "dp", "tensor"),
        P(None, "tensor", "dp"),
        P("tensor", "dp"),
        P(),
        P(),
        P(),
        P("dp", "tensor"),
        P("tensor", "dp"),
        P("tensor", "dp"),
        P(),
    )
    out_specs = (
        P(("dp", "tensor"), None),
        P(("dp", "tensor"), None),
        P(),
        P(),
        P(None, "dp", "tensor"),
        P(None, "tensor", "dp"),
        P("tensor", "dp"),
        P(),
        P(),
        P(),
        P("dp", "tensor"),
        P("tensor", "dp"),
        P("tensor", "dp"),
        P(),
    )
    return jax.shard_map(
        on_device, mesh=mesh, in_specs=in_specs, out_specs=out_specs, check_vma=False
    )
```
